32 devices in a mesh: section: 2 (over x), rows: 16 (over z, y, core).
Axes of the slice: x: 2, y: 2, z: 4, core: 2. Of those that a mesh axis runs over, the one named last changes fastest.
Arguments:
- node_latents: bfloat16 [2, 2048, 512], P(None, 'rows'), may hold values from -6 to 6
- edge_latents: bfloat16 [2, 24576, 512], P(None, 'rows'), may hold values from -6 to 6
- senders: int32 [2, 24576], P(None, 'rows'), may hold values from 0 to 2047, as said below
- receivers: int32 [2, 24576], P(None, 'rows'), may hold values from -1 to 2047, as said below
- cotangent: bfloat16 [2, 2048, 512], P(None, 'rows'), may hold values from -6 to 6
- edge_weight_in: bfloat16 [2, 1536, 512], P('section'), may hold values from -0.15625 to 0.15625
- edge_bias_in: bfloat16 [2, 512], P('section'), may hold values from -3 to 3
- edge_weight_out: bfloat16 [2, 512, 512], P('section'), may hold values from -0.25 to 0.25
- edge_bias_out: bfloat16 [2, 512], P('section'), may hold values from -3 to 3
- edge_gain: bfloat16 [2, 512], P('section'), may hold values from 0.5 to 1.5
- edge_shift: bfloat16 [2, 512], P('section'), may hold values from -2 to 2
- node_weight_in: bfloat16 [2, 1024, 512], P('section'), may hold values from -0.1875 to 0.1875
- node_bias_in: bfloat16 [2, 512], P('section'), may hold values from -3 to 3
- node_weight_out: bfloat16 [2, 512, 512], P('section'), may hold values from -0.25 to 0.25
- node_bias_out: bfloat16 [2, 512], P('section'), may hold values from -3 to 3
- node_gain: bfloat16 [2, 512], P('section'), may hold values from 0.5 to 1.5
- node_shift: bfloat16 [2, 512], P('section'), may hold values from -2 to 2
Outputs:
- node_states: float32 [2, 2, 2048, 512], P('section', None, 'rows')
- node_grads: float32 [2, 2, 2048, 512], P('section', None, 'rows')
- edge_grads: float32 [2, 2, 24576, 512], P('section', None, 'rows')
- edge_weight_in_grad: float32 [2, 1536, 512], P('section')
- edge_bias_in_grad: float32 [2, 512], P('section')
- edge_weight_out_grad: float32 [2, 512, 512], P('section')
- edge_bias_out_grad: float32 [2, 512], P('section')
- edge_gain_grad: float32 [2, 512], P('section')
- edge_shift_grad: float32 [2, 512], P('section')
- node_weight_in_grad: float32 [2, 1024, 512], P('section')
- node_bias_in_grad: float32 [2, 512], P('section')
- node_weight_out_grad: float32 [2, 512, 512], P('section')
- node_bias_out_grad: float32 [2, 512], P('section')
- node_gain_grad: float32 [2, 512], P('section')
- node_shift_grad: float32 [2, 512], P('section')
The draws below stay inside these ranges and needn't reach their ends.
Inputs may be any that keep to these rules, and one draw needn't show every extreme that they name: `receivers`: each device's block of 1536 slots along rows holds the edges into its own 128 nodes (numbers from its index times 128), at most 12 into any node, in order of receiver, followed by empty slots marked -1; in every micro-batch some device's block is full. `senders`: for every live edge, (sender - receiver) mod 2048 lies in 1 to 128 or in 1920 to 2047; on an empty slot the sender is some node without meaning.
All inputs are finite; a program needn't handle non-finite values.
Results may differ from the reference program's by a relative error of at most 0.015.
Values may be sent and summed in bfloat16 or wider, within the bound.
No kernel may reach another device: no remote copies, remote signals or barrier semaphores. Data moves between devices by JAX's collectives and lax.ppermute only.
A program may use at most 192 MiB of HBM per device.

```python
import jax
import jax.numpy as jnp
from jax import lax

D = 512
NODE_DEV = 128
MICRO = 2
DEGREE = 12
LAYERS = 2
EDGE_CAP = 1536
NODES = 2048
EDGES = 24576


def edge_layout(key):
    ranks = NODES // NODE_DEV
    key_degree, key_region, key_full, key_offset = jax.random.split(key, 4)
    region = jax.random.randint(key_region, (MICRO, ranks, 1), 0, 2)
    degree = jax.random.randint(key_degree, (MICRO, ranks, NODE_DEV), DEGREE // 3, DEGREE // 2 + 1) + DEGREE // 2 * region
    full_rank = jax.random.randint(key_full, (MICRO, 1, 1), 0, ranks)
    rank_ids = jnp.arange(ranks, dtype=jnp.int32)[None, :, None]
    degree = jnp.where(rank_ids == full_rank, DEGREE, degree).astype(jnp.int32)
    ends = jnp.cumsum(degree, axis=2).astype(jnp.int32)
    slot_ids = jnp.arange(EDGE_CAP, dtype=jnp.int32)
    owner = jax.vmap(jax.vmap(lambda limits: jnp.searchsorted(limits, slot_ids, side='right')))(ends).astype(jnp.int32)
    live = owner < NODE_DEV
    base = rank_ids * NODE_DEV
    node_clip = jnp.minimum(owner, NODE_DEV - 1)
    receiver = jnp.where(live, base + node_clip, -1)
    step = jax.random.randint(key_offset, (MICRO, ranks, EDGE_CAP), 1, 2 * NODE_DEV + 1)
    offset = jnp.where(step <= NODE_DEV, step - NODE_DEV - 1, step - NODE_DEV)
    sender = jnp.mod(base + node_clip + offset, NODES)
    return (sender.reshape(MICRO, EDGES).astype(jnp.int32), receiver.reshape(MICRO, EDGES).astype(jnp.int32))


def draw_senders(key, part):
    shared = edge_layout(key)
    return shared[0]


def draw_receivers(key, part):
    shared = edge_layout(key)
    return shared[1]


def block_scale(own_key, shape, pieces, low, largest):
    factor_of = 1.0
    for dim, shards_of in pieces:
        draws = jax.random.uniform(jax.random.fold_in(jax.random.fold_in(own_key, 6), dim), (shards_of,), jnp.float32, low / len(pieces), largest / len(pieces))
        factor_of = factor_of * jnp.repeat(jnp.exp(draws), shape[dim] // shards_of).reshape((-1,) + (1,) * (len(shape) - 1 - dim))
    return factor_of


def gaussian(own_key, dims, spread, bound, pieces=(), kind=jnp.bfloat16):
    values = spread * jax.random.normal(own_key, dims, jnp.float32)
    if pieces:
        values = values * block_scale(own_key, dims, pieces, -0.22, 0.18)
    return jnp.clip(values, -bound, bound).astype(kind)


def setup_inputs(seed: int = 0) -> dict:
    key_of = jax.random.split(jax.random.key(seed), 18)
    node_latents = gaussian(key_of[0], (MICRO, NODES, D), 1.0, 6.0, ((1, 16),))
    edge_latents = gaussian(key_of[1], (MICRO, EDGES, D), 1.0, 6.0, ((1, 16),))
    senders = draw_senders(jax.random.fold_in(key_of[17], 71), 0)
    receivers = draw_receivers(jax.random.fold_in(key_of[17], 71), 0)
    cotangent = gaussian(key_of[4], (MICRO, NODES, D), 1.0, 6.0, ((1, 16),))
    edge_weight_in = gaussian(key_of[5], (LAYERS, 3 * D, D), (3 * D) ** -0.5, 0.15625, ((0, 2),))
    edge_bias_in = gaussian(key_of[6], (LAYERS, D), 0.5, 3.0, ((0, 2),))
    edge_weight_out = gaussian(key_of[7], (LAYERS, D, D), D ** -0.5, 0.25, ((0, 2),))
    edge_bias_out = gaussian(key_of[8], (LAYERS, D), 0.5, 3.0, ((0, 2),))
    edge_gain = jnp.clip(1.0 + 0.1 * jax.random.normal(key_of[9], (LAYERS, D), jnp.float32), 0.5, 1.5).astype(jnp.bfloat16)
    edge_shift = gaussian(key_of[10], (LAYERS, D), 0.3, 2.0, ((0, 2),))
    node_weight_in = gaussian(key_of[11], (LAYERS, 2 * D, D), (2 * D) ** -0.5, 0.1875, ((0, 2),))
    node_bias_in = gaussian(key_of[12], (LAYERS, D), 0.5, 3.0, ((0, 2),))
    node_weight_out = gaussian(key_of[13], (LAYERS, D, D), D ** -0.5, 0.25, ((0, 2),))
    node_bias_out = gaussian(key_of[14], (LAYERS, D), 0.5, 3.0, ((0, 2),))
    node_gain = jnp.clip(1.0 + 0.1 * jax.random.normal(key_of[15], (LAYERS, D), jnp.float32), 0.5, 1.5).astype(jnp.bfloat16)
    node_shift = gaussian(key_of[16], (LAYERS, D), 0.3, 2.0, ((0, 2),))
    return dict(node_latents=node_latents, edge_latents=edge_latents, senders=senders, receivers=receivers, cotangent=cotangent, edge_weight_in=edge_weight_in, edge_bias_in=edge_bias_in, edge_weight_out=edge_weight_out, edge_bias_out=edge_bias_out, edge_gain=edge_gain, edge_shift=edge_shift, node_weight_in=node_weight_in, node_bias_in=node_bias_in, node_weight_out=node_weight_out, node_bias_out=node_bias_out, node_gain=node_gain, node_shift=node_shift)


@jax.custom_vjp
def low(v):
    return lax.optimization_barrier(v.astype(jnp.bfloat16)).astype(jnp.float32)

@jax.custom_vjp
def low_back(v):
    return v

def low_keep(v):
    return (low(v), None)

def low_pass(kept, grad):
    return (grad,)

def back_keep(v):
    return (v, None)

def back_low(kept, grad):
    return (low(grad),)
low.defvjp(low_keep, low_pass)
low_back.defvjp(back_keep, back_low)

def matmul(left, right):
    return jnp.dot(left, right, preferred_element_type=jnp.float32, precision=lax.Precision.HIGHEST)

def layer_norm(values, gain, shift):
    centred = values - lax.optimization_barrier(jnp.mean(values, axis=-1, keepdims=True))
    scale = lax.rsqrt(lax.optimization_barrier(jnp.mean(centred * centred, axis=-1, keepdims=True)) + 1e-05)
    return centred * scale * gain + shift

def processor_layer(params, nodes, edges, sender_ids, targets, live_mask):
    edge_weight_in, edge_bias_in, edge_weight_out, edge_bias_out, edge_gain, edge_shift, node_weight_in, node_bias_in, node_weight_out, node_bias_out, node_gain, node_shift = params
    nodes_low = low(nodes)
    joined = jnp.concatenate([low(edges), nodes_low[sender_ids], nodes_low[targets]], axis=1)
    hidden = low_back(matmul(joined, edge_weight_in) + edge_bias_in)
    active = low(jax.nn.silu(hidden))
    result = low_back(matmul(active, edge_weight_out) + edge_bias_out)
    update = live_mask[:, None] * layer_norm(result, edge_gain, edge_shift)
    summed = jax.ops.segment_sum(update, targets, num_segments=nodes.shape[0])
    node_join = jnp.concatenate([nodes_low, low(summed)], axis=1)
    node_hidden = low_back(matmul(node_join, node_weight_in) + node_bias_in)
    node_active = low(jax.nn.silu(node_hidden))
    node_result = low_back(matmul(node_active, node_weight_out) + node_bias_out)
    return (nodes + layer_norm(node_result, node_gain, node_shift), edges + update)

def reference(node_latents, edge_latents, senders, receivers, cotangent, edge_weight_in, edge_bias_in, edge_weight_out, edge_bias_out, edge_gain, edge_shift, node_weight_in, node_bias_in, node_weight_out, node_bias_out, node_gain, node_shift):
    stacked = (edge_weight_in, edge_bias_in, edge_weight_out, edge_bias_out, edge_gain, edge_shift, node_weight_in, node_bias_in, node_weight_out, node_bias_out, node_gain, node_shift)
    layer_one = tuple((item[0].astype(jnp.float32) for item in stacked))
    layer_two = tuple((item[1].astype(jnp.float32) for item in stacked))
    sums_one = [jnp.zeros(item.shape[1:], jnp.float32) for item in stacked]
    sums_two = [jnp.zeros(item.shape[1:], jnp.float32) for item in stacked]
    states_one, states_two = ([], [])
    node_first, node_second, edge_first, edge_second = ([], [], [], [])
    for batch in range(MICRO):
        live_mask = (receivers[batch] >= 0).astype(jnp.float32)
        targets = jnp.where(receivers[batch] >= 0, receivers[batch], 0).astype(jnp.int32)
        sender_ids = senders[batch].astype(jnp.int32)

        def forward(first_params, second_params, nodes, edges, node_tap, edge_tap):
            nodes_one, edges_one = processor_layer(first_params, nodes, edges, sender_ids, targets, live_mask)
            nodes_mid = low_back(low(nodes_one) + node_tap)
            edges_mid = low_back(low(edges_one) + edge_tap)
            nodes_two, unused_edges = processor_layer(second_params, nodes_mid, edges_mid, sender_ids, targets, live_mask)
            return (nodes_one, nodes_two)
        nodes = node_latents[batch].astype(jnp.float32)
        edges = edge_latents[batch].astype(jnp.float32)
        outputs, pullback = jax.vjp(forward, layer_one, layer_two, nodes, edges, jnp.zeros_like(nodes), jnp.zeros_like(edges))
        grads = pullback((jnp.zeros_like(outputs[0]), cotangent[batch].astype(jnp.float32)))
        states_one.append(outputs[0])
        states_two.append(outputs[1])
        sums_one = [total + item for total, item in zip(sums_one, grads[0])]
        sums_two = [total + item for total, item in zip(sums_two, grads[1])]
        node_first.append(grads[2])
        edge_first.append(grads[3])
        node_second.append(grads[4])
        edge_second.append(grads[5])
    node_states = jnp.stack([jnp.stack(states_one), jnp.stack(states_two)])
    node_grads = jnp.stack([jnp.stack(node_first), jnp.stack(node_second)])
    edge_grads = jnp.stack([jnp.stack(edge_first), jnp.stack(edge_second)])
    weights = [jnp.stack([one, two]) for one, two in zip(sums_one, sums_two)]
    return (node_states, node_grads, edge_grads, weights[0], weights[1], weights[2], weights[3], weights[4], weights[5], weights[6], weights[7], weights[8], weights[9], weights[10], weights[11])
```

```python
from types import SimpleNamespace

import jax
import jax.numpy as jnp
from jax import lax
from jax.experimental import pallas as pl
from jax.experimental.pallas import tpu as pltpu
from jax.sharding import PartitionSpec as P

EPSILON = 1e-05
PIECES = 8
EXTRA = 16
TILE = 512
LANES = 128
MIB = 1024 * 1024
F32 = jnp.float32
LOW = jnp.bfloat16
EDGE_IN, SENDER_IN, TARGET_IN, EDGE_OUT, NODE_IN, SUMMED_IN, NODE_OUT = range(7)
MATRICES = 7
ORDER = (SENDER_IN, TARGET_IN, EDGE_IN, EDGE_OUT, NODE_IN, SUMMED_IN, NODE_OUT)


def dot_nn(left, right):
    return jnp.dot(left, right, preferred_element_type=F32)


def dot_nt(left, right):
    return lax.dot_general(left, right, (((1,), (1,)), ((), ())), preferred_element_type=F32)


def dot_tn(left, right):
    return lax.dot_general(left, right, (((0,), (0,)), ((), ())), preferred_element_type=F32)


def silu_parts(half):
    above = 1.0 + jnp.tanh(half)
    active = half * above
    return active, above + active * (2.0 - above)


def norm_parts(values):
    centred = values - jnp.mean(values, axis=-1, keepdims=True)
    scale = lax.rsqrt(jnp.mean(centred * centred, axis=-1, keepdims=True) + EPSILON)
    return centred * scale, scale


def norm_backward(scaled, unit, scale):
    first = jnp.mean(scaled, axis=-1, keepdims=True)
    second = jnp.mean(scaled * unit, axis=-1, keepdims=True)
    return scale * (scaled - first - unit * second)


def folded(values):
    rows, columns = values.shape
    return jnp.sum(values.reshape(rows // 8, 8, columns), axis=0)


def column_sum(values):
    return jnp.sum(values, axis=0, keepdims=True)


def hot_columns(index, width):
    places = lax.broadcasted_iota(jnp.int32, (index.shape[0], width), 1)
    return jnp.where(places == index, 1.0, 0.0).astype(LOW)


def hot_rows(index, height):
    places = lax.broadcasted_iota(jnp.int32, (height, index.shape[1]), 0)
    return jnp.where(places == index, 1.0, 0.0).astype(LOW)


def block(i, size):
    if isinstance(i, int):
        return pl.ds(i * size, size)
    return pl.ds(pl.multiple_of(i * size, size), size)


def repeat(count, body, looped):
    if not looped:
        for i in range(count):
            body(i)
        return

    def step(i, carry):
        body(i)
        return carry

    lax.fori_loop(0, count, step, 0)


def each_tile(batches, slots, body, looped):
    parts = slots // TILE

    def each_part(batch):
        for part in range(parts):
            body(batch, block(part, TILE), block(batch * parts + part, TILE))

    repeat(batches, each_part, looped)


class Copies:
    def __init__(self, semaphores):
        self.semaphores = semaphores
        self.used = 0
        self.leaving = []

    def semaphore(self):
        self.used += 1
        return self.semaphores.at[self.used - 1]

    def fetch(self, source, target):
        copy = pltpu.make_async_copy(source, target, self.semaphore())
        copy.start()
        return copy

    def fetch_either(self, flag, when_set, otherwise, target):
        semaphore = self.semaphore()
        copy = pltpu.make_async_copy(when_set, target, semaphore)
        other = pltpu.make_async_copy(otherwise, target, semaphore)
        pl.when(flag)(copy.start)
        pl.when(jnp.logical_not(flag))(other.start)
        return copy

    def send(self, source, target):
        self.leaving.append(self.fetch(source, target))

    def finish(self):
        wait_all(self.leaving)


def wait_all(copies):
    for copy in copies:
        copy.wait()


def run_kernel(
    place,
    inputs,
    outputs,
    scratch,
    near_inputs=None,
    near_outputs=None,
    renewed=None,
    work=1.0,
    memory=60,
    after=None,
    section=None,
):
    groups = []
    near_inputs = dict(near_inputs or {})
    near_outputs = dict(near_outputs or {})
    if after is not None:
        near_inputs.update(tokens=tuple(after))
        near_outputs.update(token=jax.ShapeDtypeStruct((8, LANES), F32))
    arguments = [place]
    in_specs = [pl.BlockSpec(memory_space=pltpu.SMEM)]
    far = pl.BlockSpec(memory_space=pl.ANY)
    close = pl.BlockSpec(memory_space=pltpu.VMEM)
    for group, spec in ((inputs, far), (near_inputs, close)):
        for key, value in group.items():
            items = value if isinstance(value, tuple) else (value,)
            groups.append((key, len(items), isinstance(value, tuple)))
            arguments += items
            in_specs += [spec] * len(items)
    renewed = renewed or {}
    shapes = {key: jax.ShapeDtypeStruct(item.shape, item.dtype) for key, item in renewed.items()}
    made = {**shapes, **outputs, **near_outputs}
    aliases = {len(arguments) + i: i for i in range(len(renewed))}
    first_old = len(arguments)
    arguments += renewed.values()
    in_specs += [far] * len(renewed)
    out_specs = [close if key in near_outputs else far for key in made]

    def decorate(body):
        def kernel(*refs):
            named = SimpleNamespace(place=refs[0])
            used = 1
            for key, size, several in groups:
                part = refs[used : used + size]
                setattr(named, key, part if several else part[0])
                used += size
            used = first_old + len(renewed)
            for key in (*made, *scratch):
                setattr(named, key, refs[used])
                used += 1
            if after is not None:
                named.token[...] = jnp.zeros_like(named.token)
            body(named)

        call = pl.pallas_call(
            kernel,
            out_shape=list(made.values()),
            in_specs=in_specs,
            out_specs=out_specs,
            input_output_aliases=aliases,
            scratch_shapes=list(scratch.values()),
            compiler_params=pltpu.CompilerParams(vmem_limit_bytes=memory * MIB),
            cost_estimate=pl.CostEstimate(
                flops=int(work * 4e9), bytes_accessed=int(work * 8e6), transcendentals=0
            ),
            name=body.__name__,
        )
        if section is None:
            results = call(*arguments)
        else:

            def nothing(*refs):
                pass

            skip = pl.pallas_call(
                nothing,
                out_shape=list(made.values()),
                in_specs=[],
                out_specs=out_specs,
                compiler_params=pltpu.CompilerParams(vmem_limit_bytes=memory * MIB),
            )
            here = lax.axis_index("section") == section
            results = lax.cond(here, call, lambda *unused: skip(), *arguments)
        return SimpleNamespace(**dict(zip(made, results)))

    return decorate


def shape(dims, kind=LOW):
    return jax.ShapeDtypeStruct(dims, kind)


def semaphores(count):
    return pltpu.SemaphoreType.DMA((count,))


def near_sources(ref):
    return [
        ref.edge_in.at[0],
        ref.edge_in.at[1],
        ref.edge_in.at[2],
        ref.edge_out,
        ref.node_in.at[0],
        ref.node_in.at[1],
        ref.node_out,
    ]


class Weights:
    def __init__(self, ref):
        self.target = ref.weights
        self.semaphores = ref.weight_semaphores

    def fetch_near(self, ref, order):
        sources = near_sources(ref)
        for matrix in order:
            pltpu.make_async_copy(
                sources[matrix], self.target.at[matrix], self.semaphores.at[matrix]
            ).start()

    def fetch_far(self, ref, order):
        piece = self.target.shape[1] // PIECES
        mine = ref.place[1] % PIECES
        for matrix in order:
            for offset, source in enumerate(ref.far):
                rows = pl.ds(pl.multiple_of((mine ^ offset) * piece, piece), piece)
                pltpu.make_async_copy(
                    source.at[pl.ds(matrix * piece, piece)],
                    self.target.at[matrix, rows],
                    self.semaphores.at[matrix],
                ).start()

    def wait(self, *order):
        for matrix in order:
            whole = self.target.at[matrix]
            pltpu.make_async_copy(whole, whole, self.semaphores.at[matrix]).wait()

    def __getitem__(self, matrix):
        return self.target[matrix]


def weight_scratch(width):
    return dict(
        weights=pltpu.VMEM((MATRICES, width, width), LOW),
        weight_semaphores=semaphores(MATRICES),
        vectors=pltpu.VMEM((EXTRA, width), LOW),
    )


def far_vectors(ref):
    return ref.far[0].at[pl.ds(ref.far[0].shape[0] - EXTRA, EXTRA)]


def project_nodes(spread, count, weights, vectors, joint):
    width = spread.shape[1]
    sender = 0.5 * dot_nn(spread, weights[SENDER_IN])
    middle = jnp.concatenate(
        [
            spread[start + count : start + 2 * count, :]
            for start in range(0, spread.shape[0], 3 * count)
        ],
        axis=0,
    )
    target = 0.5 * (dot_nn(middle, weights[TARGET_IN]) + vectors[0:1, :])
    half = weights[EDGE_IN] * 0.5
    for batch in range(spread.shape[0] // (3 * count)):
        joint[batch, :width, :] = half
        joint[batch, width : width + 3 * count, :] = sender[
            3 * count * batch : 3 * count * (batch + 1), :
        ].astype(LOW)
        joint[batch, width + 3 * count :, :] = target[
            count * batch : count * (batch + 1), :
        ].astype(LOW)
    return middle


def forward_tile(edges, hot_senders, hot_targets, joint, weights, vectors):
    joined = jnp.concatenate([edges, hot_senders, hot_targets], axis=1)
    active, slope = silu_parts(dot_nn(joined, joint))
    active = active.astype(LOW)
    unit, scale = norm_parts(dot_nn(active, weights[EDGE_OUT]) + vectors[1:2, :])
    return active, slope, unit, scale


def sum_updates(targets, units, vectors, count):
    hot = hot_rows(targets, count)
    degree = jnp.sum(hot.astype(F32), axis=1, keepdims=True)
    return vectors[2:3, :] * dot_nn(hot, units) + vectors[3:4, :] * degree


def node_forward(nodes, summed, weights, vectors):
    hidden = dot_nn(nodes, weights[NODE_IN]) + dot_nn(summed, weights[SUMMED_IN])
    active, slope = silu_parts(0.5 * (hidden + vectors[4:5, :]))
    active = active.astype(LOW)
    unit, scale = norm_parts(dot_nn(active, weights[NODE_OUT]) + vectors[5:6, :])
    states = nodes.astype(F32) + unit * vectors[6:7, :] + vectors[7:8, :]
    return states, active, slope, unit, scale


def node_backward(incoming, slope, unit, scale, weights, vectors):
    result_grad = norm_backward(incoming * vectors[6:7, :], unit, scale).astype(LOW)
    hidden_grad = (dot_nt(result_grad, weights[NODE_OUT]) * (0.5 * slope)).astype(LOW)
    base = incoming + dot_nt(hidden_grad, weights[NODE_IN])
    return result_grad, hidden_grad, base, dot_nt(hidden_grad, weights[SUMMED_IN])


def node_weight_grads(pack, nodes, summed, active, result_grad, hidden_grad, incoming, unit):
    width = nodes.shape[1]
    pack[:width, :] = dot_tn(nodes, hidden_grad).astype(LOW)
    pack[width : 2 * width, :] = dot_tn(summed, hidden_grad).astype(LOW)
    pack[2 * width : 3 * width, :] = dot_tn(active, result_grad).astype(LOW)
    sums = [
        column_sum(hidden_grad.astype(F32)),
        column_sum(result_grad.astype(F32)),
        column_sum(incoming * unit),
        column_sum(incoming),
    ]
    pack[3 * width :, :] = extra_rows(sums)


def extra_rows(sums):
    zeros = jnp.zeros((EXTRA - len(sums), sums[0].shape[1]), F32)
    return jnp.concatenate([*sums, zeros], axis=0).astype(LOW)


def backward_tile(incoming, slope, unit, scale, half_out, vectors):
    result_grad = norm_backward(incoming * vectors[2:3, :], unit, scale)
    low_grad = result_grad.astype(LOW)
    hidden_grad = (dot_nt(low_grad, half_out) * slope).astype(LOW)
    sums = (folded(result_grad), folded(incoming * unit), folded(incoming))
    return low_grad, hidden_grad, sums


def add_each(left, right):
    return tuple(a + b for a, b in zip(left, right))


def scattered(rows, hidden_grad, count):
    senders = dot_nn(hot_rows(rows[0:1, :], 3 * count), hidden_grad)
    targets = dot_nn(hot_rows(rows[1:2, :], count), hidden_grad)
    return senders, targets


def return_to_nodes(senders, targets, weights):
    count = targets.shape[0]
    grad = dot_nt(senders, weights[SENDER_IN])
    own = grad[count : 2 * count, :] + dot_nt(targets, weights[TARGET_IN])
    return grad[:count, :].astype(LOW), grad[2 * count :, :].astype(LOW), own


def send_pack(copies, row, pack, keep, send):
    half = (pack.shape[0] - EXTRA) // 2
    bit = row % 2
    for out, place in ((keep, bit), (send, 1 - bit)):
        rows = pl.ds(pl.multiple_of(place * half, half), half)
        copies.send(pack.at[rows], out.at[pl.ds(0, half)])
        copies.send(pack.at[pl.ds(2 * half, EXTRA)], out.at[pl.ds(half, EXTRA)])


def position_inputs(positions, halo, nodes, edges):
    return dict(rows=positions, spreads=(*halo, nodes), edges=edges)


def turned(rows):
    return jnp.transpose(rows.astype(F32)).astype(jnp.int32)


def spread_rows(ref, batch, count):
    odd = ref.place[1] % 2
    starts = ((3 * batch + 2 - 2 * odd) * count, (3 * batch + 2 * odd) * count)
    return [pl.ds(pl.multiple_of(start, count), count) for start in starts] + [
        pl.ds((3 * batch + 1) * count, count)
    ]


def fetch_spread(copies, ref, batches):
    count = ref.spreads[0].shape[1]
    return [
        copies.fetch(source.at[batch], ref.spread.at[rows])
        for batch in range(batches)
        for source, rows in zip(ref.spreads, spread_rows(ref, batch, count))
    ]


def by_parity(ref, below, above):
    odd = ref.place[1] % 2 == 1
    return jnp.where(odd, below, above), jnp.where(odd, above, below)


def layer_one(far, weights, place, positions, halo, nodes, edges):
    batches, count, width = nodes.shape
    slots = edges.shape[1]
    picked = batches
    chosen = range(batches)
    outputs = dict(
        states_low_out=shape((batches, count, width)), edges_out=shape((batches, slots, width))
    )
    if not far:
        outputs.update(
            states_out=shape((batches, count, width), F32),
            kept_out=shape((batches, 3, slots, width)),
            scales_out=shape((batches, slots, LANES), F32),
            node_kept_out=shape((batches, 3, count, width), F32),
            node_kept_low_out=shape((batches, 2, count, width)),
        )
    scratch = dict(
        **weight_scratch(width),
        joint=pltpu.VMEM((picked, 2 * width, width), LOW),
        spread=pltpu.VMEM((picked * 3 * count, width), LOW),
        edge_buffer=pltpu.VMEM((picked, slots, width), LOW),
        column_buffer=pltpu.VMEM((picked, slots, 8), jnp.int32),
        row_buffer=pltpu.VMEM((picked, 8, slots), jnp.int32),
        edges_new=pltpu.VMEM((picked, slots, width), LOW),
        summed=pltpu.VMEM((picked * count, width), LOW),
        states=pltpu.VMEM((picked, count, width), F32),
        states_low=pltpu.VMEM((picked, count, width), LOW),
        kept=pltpu.VMEM((picked, 3, slots, width), LOW),
        scales=pltpu.VMEM((picked, slots, LANES), F32),
        node_kept=pltpu.VMEM((picked, 3, count, width), F32),
        node_kept_low=pltpu.VMEM((picked, 2, count, width), LOW),
        semaphores=semaphores(48),
    )

    def work(ref):
        copies = Copies(ref.semaphores)
        weights = Weights(ref)
        first = [copies.fetch(far_vectors(ref) if far else ref.vectors_in, ref.vectors)]
        second = []
        first += fetch_spread(copies, ref, batches)
        fetch = weights.fetch_far if far else weights.fetch_near
        fetch(ref, ORDER[:3])
        for i, batch in enumerate(chosen):
            second.append(
                [
                    copies.fetch(ref.edges.at[batch], ref.edge_buffer.at[i]),
                    copies.fetch(ref.rows.at[batch], ref.row_buffer.at[i]),
                ]
            )
            if i == 0:
                fetch(ref, ORDER[3:])
        wait_all(first)
        vectors = ref.vectors[...].astype(F32)
        weights.wait(SENDER_IN, TARGET_IN, EDGE_IN)
        middle = project_nodes(ref.spread[...], count, weights, vectors, ref.joint)
        weights.wait(EDGE_OUT)
        for batch in range(batches):
            wait_all(second[batch])
            ref.column_buffer[batch] = turned(ref.row_buffer[batch])

        def edge_tile(batch, tile, _):
            index = ref.column_buffer[batch, tile, :]
            latents = ref.edge_buffer[batch, tile, :]
            active, slope, unit, scale = forward_tile(
                latents,
                hot_columns(index[:, 0:1], 3 * count),
                hot_columns(index[:, 1:2], count),
                ref.joint[batch],
                weights,
                vectors,
            )
            live = (index[:, 1:2] >= 0).astype(F32)
            update = (unit * vectors[2:3, :] + vectors[3:4, :]) * live
            ref.edges_new[batch, tile, :] = (latents.astype(F32) + update).astype(LOW)
            ref.kept[batch, 2, tile, :] = unit.astype(LOW)
            if not far:
                ref.kept[batch, 0, tile, :] = active
                ref.kept[batch, 1, tile, :] = slope.astype(LOW)
                ref.scales[batch, tile, :] = jnp.broadcast_to(scale, (TILE, LANES))

        def sum_batch(batch):
            targets = ref.row_buffer[batch, 1:2, :]
            summed = sum_updates(targets, ref.kept[batch, 2], vectors, count)
            ref.summed[block(batch, count), :] = summed.astype(LOW)

        if far:
            each_tile(batches, slots, edge_tile, True)
            repeat(batches, sum_batch, True)
        parts = slots // TILE
        for batch in range(batches):
            if not far:
                for part in range(parts):
                    edge_tile(batch, block(part, TILE), None)
            copies.send(ref.edges_new.at[batch], ref.edges_out.at[batch])
            if not far:
                copies.send(ref.kept.at[batch], ref.kept_out.at[batch])
                copies.send(ref.scales.at[batch], ref.scales_out.at[batch])
                sum_batch(batch)
        summed = ref.summed[...]
        weights.wait(NODE_IN, SUMMED_IN, NODE_OUT)
        states, active, slope, unit, scale = node_forward(middle, summed, weights, vectors)
        for i, batch in enumerate(chosen):
            rows = slice(i * count, (i + 1) * count)
            ref.states[i] = states[rows, :]
            ref.states_low[i] = states[rows, :].astype(LOW)
            copies.send(ref.states_low.at[i], ref.states_low_out.at[batch])
            if not far:
                copies.send(ref.states.at[i], ref.states_out.at[batch])
                ref.node_kept[i, 0] = slope[rows, :]
                ref.node_kept[i, 1] = unit[rows, :]
                ref.node_kept[i, 2] = jnp.broadcast_to(scale[rows, :], (count, width))
                ref.node_kept_low[i, 0] = summed[rows, :]
                ref.node_kept_low[i, 1] = active[rows, :]
                copies.send(ref.node_kept.at[i], ref.node_kept_out.at[batch])
                copies.send(ref.node_kept_low.at[i], ref.node_kept_low_out.at[batch])
        copies.finish()

    @run_kernel(
        place,
        dict(**weights, **position_inputs(positions, halo, nodes, edges)),
        outputs,
        scratch,
        section=1 if far else 0,
    )
    def layer_one_forward(ref):
        work(ref)

    return layer_one_forward


def layer_two(second, weights, place, positions, halo, nodes, edges, cotangent):
    batches, count, width = nodes.shape
    slots = edges.shape[1]
    every = batches * slots
    nodes_shape = (batches * count, width)
    outputs = dict(
        edge_low_out=shape((every, width)),
        base_out=shape(nodes_shape, F32),
        to_pair_out=shape(nodes_shape),
        to_other_out=shape(nodes_shape),
    )
    if second:
        outputs.update(
            states_out=shape(nodes_shape, F32),
            node_keep_out=shape((3 * width // 2 + EXTRA, width)),
            node_send_out=shape((3 * width // 2 + EXTRA, width)),
            edge_keep_out=shape((2 * width + EXTRA, width)),
            edge_send_out=shape((2 * width + EXTRA, width)),
        )
    all_low = pltpu.VMEM((every, width), LOW)
    scratch = dict(
        **weight_scratch(width),
        half_out=pltpu.VMEM((width, width), LOW),
        summed=pltpu.VMEM(nodes_shape, LOW),
        sums=pltpu.VMEM((3, 8, width), F32),
        senders=pltpu.VMEM((batches * 3 * count, width), LOW),
        targets=pltpu.VMEM(nodes_shape, F32),
        total=pltpu.VMEM((2, width, width), F32),
        joint=pltpu.VMEM((batches, 2 * width, width), LOW),
        spread=pltpu.VMEM((batches * 3 * count, width), LOW),
        edge_buffer=all_low,
        column_buffer=pltpu.VMEM((batches, slots, 8), jnp.int32),
        row_buffer=pltpu.VMEM((batches, 8, slots), jnp.int32),
        cotangent_buffer=pltpu.VMEM((batches * count, width), LOW),
        hot_targets=pltpu.VMEM((every, count), LOW),
        active_all=all_low,
        slope_all=all_low,
        unit_all=all_low,
        scales=pltpu.VMEM((every, LANES), F32),
        states=pltpu.VMEM(nodes_shape, F32),
        base=pltpu.VMEM(nodes_shape, F32),
        summed_grad=pltpu.VMEM(nodes_shape, LOW),
        result_grads=all_low,
        hidden_grads=all_low,
        edge_low=all_low,
        to_pair=pltpu.VMEM(nodes_shape, LOW),
        to_other=pltpu.VMEM(nodes_shape, LOW),
        node_pack=pltpu.VMEM((3 * width + EXTRA, width), LOW),
        edge_pack=pltpu.VMEM((4 * width + EXTRA, width), LOW),
        semaphores=semaphores(48),
    )
    inputs = dict(
        **weights, **position_inputs(positions, halo, nodes, edges), cotangent=cotangent
    )

    def work(ref):
        copies = Copies(ref.semaphores)
        weights = Weights(ref)
        first = [copies.fetch(ref.vectors_in if second else far_vectors(ref), ref.vectors)]
        first += fetch_spread(copies, ref, batches)
        fetch = weights.fetch_near if second else weights.fetch_far
        fetch(ref, ORDER[:3])
        loads = []
        for batch in range(batches):
            rows = pl.ds(batch * slots, slots)
            loads.append(
                [
                    copies.fetch(ref.edges.at[batch], ref.edge_buffer.at[rows]),
                    copies.fetch(ref.rows.at[batch], ref.row_buffer.at[batch]),
                ]
            )
            if batch == 0:
                fetch(ref, ORDER[3:])
        third = [
            copies.fetch(
                ref.cotangent.at[batch], ref.cotangent_buffer.at[pl.ds(batch * count, count)]
            )
            for batch in range(batches)
        ]
        wait_all(first)
        vectors = ref.vectors[...].astype(F32)
        weights.wait(SENDER_IN, TARGET_IN, EDGE_IN)
        middle = project_nodes(ref.spread[...], count, weights, vectors, ref.joint)
        weights.wait(EDGE_OUT)
        ref.half_out[...] = weights[EDGE_OUT] * 0.5
        for batch in range(batches):
            wait_all(loads[batch])
            ref.column_buffer[batch] = turned(ref.row_buffer[batch])

        def forward(batch, tile, place):
            index = ref.column_buffer[batch, tile, :]
            hot_targets = hot_columns(index[:, 1:2], count)
            active, slope, unit, scale = forward_tile(
                ref.edge_buffer[place, :],
                hot_columns(index[:, 0:1], 3 * count),
                hot_targets,
                ref.joint[batch],
                weights,
                vectors,
            )
            ref.hot_targets[place, :] = hot_targets
            if second:
                ref.active_all[place, :] = active
            ref.slope_all[place, :] = slope.astype(LOW)
            ref.unit_all[place, :] = unit.astype(LOW)
            ref.scales[place, :] = jnp.broadcast_to(scale, (TILE, LANES))

        def sum_batch(batch):
            units = ref.unit_all[block(batch, slots), :]
            targets = ref.row_buffer[batch, 1:2, :]
            summed = sum_updates(targets, units, vectors, count)
            ref.summed[block(batch, count), :] = summed.astype(LOW)

        each_tile(batches, slots, forward, second)
        repeat(batches, sum_batch, second)
        summed = ref.summed[...]
        wait_all(third)
        weights.wait(NODE_IN, SUMMED_IN, NODE_OUT)
        states, active, slope, unit, scale = node_forward(middle, summed, weights, vectors)
        ref.states[...] = states
        incoming = ref.cotangent_buffer[...].astype(F32)
        result_grad, hidden_grad, base, summed_grad = node_backward(
            incoming, slope, unit, scale, weights, vectors
        )
        ref.summed_grad[...] = summed_grad.astype(LOW)
        ref.base[...] = base
        if second:
            node_weight_grads(
                ref.node_pack, middle, summed, active, result_grad, hidden_grad, incoming, unit
            )
        if second:
            ref.sums[...] = jnp.zeros_like(ref.sums)

        def backward(batch, tile, place):
            incoming = dot_nn(
                ref.hot_targets[place, :], ref.summed_grad[block(batch, count), :]
            )
            low_grad, hidden_grad, more = backward_tile(
                incoming,
                ref.slope_all[place, :].astype(F32),
                ref.unit_all[place, :].astype(F32),
                jnp.concatenate([ref.scales[place, :]] * (width // LANES), axis=1),
                ref.half_out[...],
                vectors,
            )
            edge_grad = dot_nt(hidden_grad, weights[EDGE_IN])
            if second:
                for i, item in enumerate(more):
                    ref.sums[i] += item
                ref.result_grads[place, :] = low_grad
            ref.hidden_grads[place, :] = hidden_grad
            ref.edge_low[place, :] = edge_grad.astype(LOW)

        def scatter(batch):
            rows = block(batch, slots)
            here = block(batch, count)
            to_senders, to_targets = scattered(
                ref.row_buffer[batch], ref.hidden_grads[rows, :], count
            )
            to_senders = to_senders.astype(LOW)
            if second:
                ref.senders[block(batch, 3 * count), :] = to_senders
                ref.targets[here, :] = to_targets
            below, above, own = return_to_nodes(to_senders, to_targets.astype(LOW), weights)
            below, above = by_parity(ref, below, above)
            ref.to_pair[here, :] = below
            ref.to_other[here, :] = above
            ref.base[here, :] += own

        parts = slots // TILE
        if second:
            each_tile(batches, slots, backward, True)
            copies.send(ref.edge_low, ref.edge_low_out)
            repeat(batches, scatter, True)
        for batch in range(0 if second else batches):
            for part in range(parts):
                backward(batch, None, block(batch * parts + part, TILE))
            rows = block(batch, slots)
            copies.send(ref.edge_low.at[rows], ref.edge_low_out.at[rows])
            scatter(batch)
        copies.send(ref.to_pair, ref.to_pair_out)
        copies.send(ref.to_other, ref.to_other_out)
        copies.send(ref.base, ref.base_out)
        if second:
            copies.send(ref.states, ref.states_out)
            ref.total[...] = jnp.zeros_like(ref.total)

            def add_rows(i):
                rows = block(i, TILE)
                ref.total[0] += dot_tn(ref.edge_buffer[rows, :], ref.hidden_grads[rows, :])
                ref.total[1] += dot_tn(ref.active_all[rows, :], ref.result_grads[rows, :])

            repeat(every // TILE, add_rows, True)
            edge_weight_grads(
                ref.edge_pack,
                ref.total[0],
                ref.total[1],
                ref.spread[...],
                middle,
                ref.senders[...],
                ref.targets[...],
                [ref.sums[i] for i in range(3)],
            )
            send_pack(copies, ref.place[1], ref.edge_pack, ref.edge_keep_out, ref.edge_send_out)
            send_pack(copies, ref.place[1], ref.node_pack, ref.node_keep_out, ref.node_send_out)
        copies.finish()

    @run_kernel(place, inputs, outputs, scratch, work=6.0, section=1 if second else 0)
    def layer_two_both(ref):
        work(ref)

    return layer_two_both


def edge_weight_grads(pack, edge_part, active_part, spread, middle, senders, targets, sums):
    width = spread.shape[1]
    pack[:width, :] = edge_part.astype(LOW)
    pack[width : 2 * width, :] = dot_tn(spread, senders).astype(LOW)
    pack[2 * width : 3 * width, :] = dot_tn(middle, targets.astype(LOW)).astype(LOW)
    pack[3 * width : 4 * width, :] = active_part.astype(LOW)
    pack[4 * width :, :] = extra_rows([column_sum(targets), *map(column_sum, sums)])


def layer_one_back(weights, place, positions, halo, nodes, edges, near, two, packs, second):
    batches, count, width = nodes.shape
    slots = edges.shape[1]
    every = batches * slots
    nodes_shape = (batches * count, width)
    loaded = dict(
        base=second[0],
        from_pair=second[1],
        from_other=second[2],
        node_kept=near.node_kept_out,
        node_kept_low=near.node_kept_low_out,
    )
    outputs = dict(hidden_out=shape((every, width)))
    all_low = pltpu.VMEM((every, width), LOW)
    nodes_low = pltpu.VMEM(nodes_shape, LOW)
    scratch = dict(
        **weight_scratch(width),
        half_out=pltpu.VMEM((width, width), LOW),
        spread=pltpu.VMEM((batches * 3 * count, width), LOW),
        edge_buffer=all_low,
        column_buffer=pltpu.VMEM((batches, slots, 8), jnp.int32),
        row_buffer=pltpu.VMEM((batches, 8, slots), jnp.int32),
        kept=pltpu.VMEM((3, every, width), LOW),
        scales=pltpu.VMEM((every, LANES), F32),
        edge_low=all_low,
        summed_grad=nodes_low,
        to_pair=nodes_low,
        to_other=nodes_low,
        result_grads=all_low,
        hidden_grads=all_low,
        node_pack=pltpu.VMEM((3 * width + EXTRA, width), LOW),
        edge_pack=pltpu.VMEM((4 * width + EXTRA, width), LOW),
        semaphores=semaphores(64),
        **{key: pltpu.VMEM(value.shape, value.dtype) for key, value in loaded.items()},
    )
    renewed = dict(
        node_keep_out=packs.node_keep_out,
        node_send_out=packs.node_send_out,
        edge_keep_out=packs.edge_keep_out,
        edge_send_out=packs.edge_send_out,
        base_out=packs.base_out,
        to_pair_out=packs.to_pair_out,
        to_other_out=packs.to_other_out,
    )
    inputs = dict(
        **weights,
        **position_inputs(positions, halo, nodes, edges),
        loads=tuple(loaded.values()),
        edge_low_in=two.edge_low_out,
        scales_in=near.scales_out,
        kept_in=near.kept_out,
    )

    def stacked(items):
        return jnp.concatenate(items, axis=0)

    def work(ref):
        copies = Copies(ref.semaphores)
        weights = Weights(ref)
        first = [copies.fetch(ref.vectors_in, ref.vectors)]
        first += [copies.fetch(source, getattr(ref, key)) for key, source in zip(loaded, ref.loads)]
        weights.fetch_near(ref, (NODE_OUT, NODE_IN, SUMMED_IN))
        first += fetch_spread(copies, ref, batches)
        second = []
        third = []
        for batch in range(batches):
            rows = pl.ds(batch * slots, slots)
            second.append(
                [
                    copies.fetch(ref.edge_low_in.at[rows], ref.edge_low.at[rows]),
                    copies.fetch(ref.scales_in.at[batch], ref.scales.at[rows]),
                    copies.fetch(ref.kept_in.at[batch], ref.kept.at[:, rows]),
                    copies.fetch(ref.rows.at[batch], ref.row_buffer.at[batch]),
                ]
            )
            if batch == 0:
                weights.fetch_near(ref, (EDGE_OUT, SENDER_IN, TARGET_IN))
            third.append(copies.fetch(ref.edges.at[batch], ref.edge_buffer.at[rows]))
        wait_all(first)
        vectors = ref.vectors[...].astype(F32)
        weights.wait(NODE_OUT, NODE_IN, SUMMED_IN)
        middle = stacked(
            [
                ref.spread[(3 * batch + 1) * count : (3 * batch + 2) * count, :]
                for batch in range(batches)
            ]
        )
        incoming = (
            ref.base[...] + ref.from_pair[...].astype(F32) + ref.from_other[...].astype(F32)
        )
        incoming = incoming.astype(LOW).astype(F32)
        slope, unit, scale = (
            stacked([ref.node_kept[batch, i] for batch in range(batches)]) for i in range(3)
        )
        summed, active = (
            stacked([ref.node_kept_low[batch, i] for batch in range(batches)]) for i in range(2)
        )
        result_grad, hidden_grad, base, summed_grad = node_backward(
            incoming, slope, unit, scale, weights, vectors
        )
        ref.summed_grad[...] = summed_grad.astype(LOW)
        ref.base[...] = base
        node_weight_grads(
            ref.node_pack, middle, summed, active, result_grad, hidden_grad, incoming, unit
        )
        weights.wait(EDGE_OUT, SENDER_IN, TARGET_IN)
        ref.half_out[...] = weights[EDGE_OUT] * 0.5
        sums = None
        senders = []
        targets = []
        for batch in range(batches):
            wait_all(second[batch])
            ref.column_buffer[batch] = turned(ref.row_buffer[batch])
            nodes_here = slice(batch * count, (batch + 1) * count)
            for part in range(slots // TILE):
                tile, place = block(part, TILE), block(batch * (slots // TILE) + part, TILE)
                hot = hot_columns(ref.column_buffer[batch, tile, 1:2], count)
                incoming = ref.edge_low[place, :].astype(F32) + dot_nn(
                    hot, ref.summed_grad[nodes_here, :]
                )
                low_grad, hidden_grad, more = backward_tile(
                    incoming,
                    ref.kept[1, place, :].astype(F32),
                    ref.kept[2, place, :].astype(F32),
                    jnp.concatenate([ref.scales[place, :]] * (width // LANES), axis=1),
                    ref.half_out[...],
                    vectors,
                )
                sums = more if sums is None else add_each(sums, more)
                ref.result_grads[place, :] = low_grad
                ref.hidden_grads[place, :] = hidden_grad
            rows = slice(batch * slots, (batch + 1) * slots)
            to_senders, to_targets = scattered(
                ref.row_buffer[batch], ref.hidden_grads[rows, :], count
            )
            senders.append(to_senders.astype(LOW))
            targets.append(to_targets)
        wait_all(third)
        copies.send(ref.hidden_grads, ref.hidden_out)
        edge_weight_grads(
            ref.edge_pack,
            dot_tn(ref.edge_buffer[...], ref.hidden_grads[...]),
            dot_tn(ref.kept[0], ref.result_grads[...]),
            ref.spread[...],
            middle,
            stacked(senders),
            stacked(targets),
            sums,
        )
        send_pack(copies, ref.place[1], ref.edge_pack, ref.edge_keep_out, ref.edge_send_out)
        send_pack(copies, ref.place[1], ref.node_pack, ref.node_keep_out, ref.node_send_out)
        for batch in range(batches):
            nodes_here = slice(batch * count, (batch + 1) * count)
            below, above, own = return_to_nodes(
                senders[batch], targets[batch].astype(LOW), weights
            )
            below, above = by_parity(ref, below, above)
            ref.to_pair[nodes_here, :] = below
            ref.to_other[nodes_here, :] = above
            ref.base[nodes_here, :] += own
        copies.send(ref.to_pair, ref.to_pair_out)
        copies.send(ref.to_other, ref.to_other_out)
        copies.send(ref.base, ref.base_out)
        copies.finish()

    @run_kernel(place, inputs, outputs, scratch, renewed=renewed, work=6.0)
    def layer_one_backward(ref):
        pl.when(ref.place[0] == 0)(lambda: work(ref))

    return layer_one_backward


def edge_outputs(weights, place, near_low, far_low, hidden, after):
    every, width = near_low.shape
    scratch = dict(
        edge_weight=pltpu.VMEM((width, width), LOW),
        edge_buffer=pltpu.VMEM((every, width), LOW),
        hidden_buffer=pltpu.VMEM((every, width), LOW),
        full=pltpu.VMEM((every, width), F32),
        semaphores=semaphores(2 * every // TILE + every // TILE + 1),
    )

    @run_kernel(
        place,
        dict(
            edge_in=weights["edge_in"],
            near_low=near_low,
            far_low=far_low,
            hidden=hidden,
        ),
        dict(edge_grads_out=shape((every, width), F32)),
        scratch,
        work=0.05,
        after=after,
    )
    def edge_gradients(ref):
        first_section = ref.place[0] == 0
        copies = Copies(ref.semaphores)
        weight = copies.fetch(ref.edge_in.at[0], ref.edge_weight)
        arriving = [
            [
                copies.fetch(ref.hidden.at[tile], ref.hidden_buffer.at[tile]),
                copies.fetch_either(
                    first_section,
                    ref.near_low.at[tile],
                    ref.far_low.at[tile],
                    ref.edge_buffer.at[tile],
                ),
            ]
            for tile in [block(i, TILE) for i in range(every // TILE)]
        ]
        weight.wait()
        for tile, loads in zip([block(i, TILE) for i in range(every // TILE)], arriving):
            wait_all(loads)
            edge_in = ref.edge_buffer[tile, :].astype(F32)

            @pl.when(ref.place[0] == 0)
            def _():
                more = dot_nt(ref.hidden_buffer[tile, :], ref.edge_weight[...])
                ref.full[tile, :] = edge_in + more

            @pl.when(ref.place[0] == 1)
            def _():
                ref.full[tile, :] = edge_in

            copies.send(ref.full.at[tile], ref.edge_grads_out.at[tile])
        copies.finish()

    return edge_gradients.edge_grads_out, edge_gradients.token


def node_outputs(place, near, far_two, back, received, after):
    dims = far_two.states_out.shape
    full = pltpu.VMEM(dims, F32)
    low = pltpu.VMEM(dims, LOW)

    @run_kernel(
        place,
        dict(
            parts=(back.base_out, *received),
            near=near.states_out.reshape(dims),
            far=far_two.states_out,
        ),
        dict(grads_out=shape(dims, F32), states_out=shape(dims, F32)),
        dict(base=full, below=low, above=low, states=full, semaphores=semaphores(6)),
        work=0.02,
        after=after,
    )
    def finish_nodes(ref):
        first_section = ref.place[0] == 0
        copies = Copies(ref.semaphores)
        states = copies.fetch_either(first_section, ref.near, ref.far, ref.states)
        wait_all(
            [copies.fetch(*pair) for pair in zip(ref.parts, (ref.base, ref.below, ref.above))]
        )
        total = ref.base[...] + ref.below[...].astype(F32) + ref.above[...].astype(F32)
        ref.base[...] = jnp.where(first_section, total, total.astype(LOW).astype(F32))
        copies.send(ref.base, ref.grads_out)
        states.wait()
        copies.send(ref.states, ref.states_out)
        copies.finish()

    return finish_nodes


def weight_pieces(weights, vectors, place):
    width = weights["edge_out"].shape[1]
    piece = width // PIECES
    rows = MATRICES * piece + EXTRA

    @run_kernel(
        place,
        dict(**weights, lines=vectors),
        dict(
            own_out=shape((rows, width)),
            other_out=shape((rows, width)),
            third_out=shape((rows, width)),
            vectors_out=shape((EXTRA, width)),
        ),
        dict(
            own=pltpu.VMEM((rows, width), LOW),
            other=pltpu.VMEM((rows, width), LOW),
            third=pltpu.VMEM((rows, width), LOW),
            single=pltpu.VMEM((len(vectors), 1, width), LOW),
            semaphores=semaphores(3 * MATRICES + len(vectors) + 4),
        ),
        work=0.02,
    )
    def weight_piece(ref):
        copies = Copies(ref.semaphores)
        mine = ref.place[1] % PIECES
        sources = near_sources(ref)
        lines = [copies.fetch(line, ref.single.at[i]) for i, line in enumerate(ref.lines)]
        arriving = []
        for buffer, offset in ((ref.own, 0), (ref.other, 6), (ref.third, 2)):
            place = pl.ds(pl.multiple_of((mine ^ offset) * piece, piece), piece)
            for matrix, source in enumerate(sources):
                target = buffer.at[pl.ds(matrix * piece, piece)]
                arriving.append(copies.fetch(source.at[place], target))
        wait_all(lines)
        extra = extra_rows([ref.single[i].astype(F32) for i in range(len(lines))])
        for buffer in (ref.own, ref.other, ref.third):
            buffer[MATRICES * piece :, :] = extra
        wait_all(arriving)
        copies.send(ref.own, ref.own_out)
        copies.send(ref.other, ref.other_out)
        copies.send(ref.third, ref.third_out)
        copies.send(ref.own.at[pl.ds(MATRICES * piece, EXTRA)], ref.vectors_out)
        copies.finish()

    return weight_piece


def along_rows(value, route):
    length = lax.axis_size("rows")
    return lax.ppermute(value, "rows", [(i, route(i)) for i in range(length)])


def neighbours(value, section=None, other=None):
    length = lax.axis_size("rows")
    pair = [(i, i ^ 1) for i in range(length)]
    beside = [(i, (i + 1 if i % 2 else i - 1) % length) for i in range(length)]
    axes = "rows"
    if section is not None:
        axes = ("section", "rows")
        start = section * length
        pair, beside = (
            [(start + one, start + two) for one, two in pairs] for pairs in (pair, beside)
        )
    return (
        lax.ppermute(value, axes, pair),
        lax.ppermute(value if other is None else other, axes, beside),
    )


def within(value, route, section):
    length = lax.axis_size("rows")
    start = section * length
    pairs = [(start + i, start + route(i)) for i in range(length)]
    return lax.ppermute(value, ("section", "rows"), pairs)


def across(value, mask):
    return along_rows(value, lambda i: i ^ mask)


def exchange(value, stage):
    return along_rows(value, lambda i: i ^ (1 << stage[i % 2]))


def stage_bit(row, stage):
    return (row >> jnp.where(row % 2 == 0, stage[0], stage[1])) & 1


def add_part(kept, received, place, stage, other, after=None):
    rows, width = kept.shape
    half = (rows - EXTRA) // 2

    @run_kernel(
        place,
        {},
        {},
        {},
        near_inputs=dict(kept=kept, received=received),
        near_outputs=dict(sum_out=shape((half + EXTRA, width))),
        work=0.01,
        memory=8,
        after=after,
    )
    def add_halves(ref):
        bit = stage_bit(ref.place[1], stage)
        part = pl.ds(pl.multiple_of((1 - bit if other else bit) * half, EXTRA), half)
        total = ref.kept[part, :].astype(F32) + ref.received[part, :].astype(F32)
        ref.sum_out[:half, :] = total.astype(LOW)
        total = ref.kept[2 * half :, :].astype(F32) + ref.received[2 * half :, :].astype(F32)
        ref.sum_out[half:, :] = total.astype(LOW)

    return add_halves


def add_last(kept, received, place, after):
    rows, width = kept.shape
    rows = rows - EXTRA

    @run_kernel(
        place,
        {},
        {},
        {},
        near_inputs=dict(kept=kept, received=received),
        near_outputs=dict(own_out=shape((rows, width)), extra_out=shape((EXTRA, width), F32)),
        work=0.01,
        memory=8,
        after=after,
    )
    def add_chunk(ref):
        total = ref.kept[...].astype(F32) + ref.received[...].astype(F32)
        ref.own_out[...] = total[:rows, :].astype(LOW)
        ref.extra_out[...] = total[rows:, :]

    return add_chunk


def join(own, received, place, stage, after):
    rows, width = own.shape

    @run_kernel(
        place,
        {},
        {},
        {},
        near_inputs=dict(own=own, received=received),
        near_outputs=dict(joined_out=shape((2 * rows, width))),
        work=0.01,
        memory=8,
        after=after,
    )
    def join_halves(ref):
        bit = stage_bit(ref.place[1], stage)
        for source, side in ((ref.own, bit), (ref.received, 1 - bit)):
            ref.joined_out[pl.ds(pl.multiple_of(side * rows, EXTRA), rows), :] = source[...]

    return join_halves


def unpack(pairs, place, stage, flipped, previous, extras=()):
    width = pairs[0][0].shape[1]
    quarters = [pair[0].shape[0] for pair in pairs]
    renewed = {}
    outputs = {}
    for i, quarter in enumerate(quarters):
        outputs[f"inner_{i}"] = shape((4 * quarter - width, width), F32)
        outputs[f"outer_{i}"] = shape((width, width), F32)
    if previous is not None:
        renewed = {key: getattr(previous, key) for key in outputs}
        outputs = {}
    lines = {f"line_{i}": shape((1, width), F32) for i in range(4 * len(extras))}
    chunks = tuple(chunk for pair in pairs for chunk in pair)

    @run_kernel(
        place,
        {},
        outputs,
        dict(
            full=pltpu.VMEM((2 * sum(quarters), width), F32),
            semaphores=semaphores(4 * len(pairs)),
        ),
        near_inputs=dict(chunks=chunks, extras=extras),
        near_outputs=lines,
        renewed=renewed,
        work=0.02,
        memory=16,
        after=(),
    )
    def widen_sums(ref):
        for i in range(len(lines)):
            getattr(ref, f"line_{i}")[...] = ref.extras[i // 4][i % 4 : i % 4 + 1, :]
        step = EXTRA * 8
        moves = []
        base = 0
        for i, chunk in enumerate(ref.chunks):
            quarter = chunk.shape[0]
            for row in range(0, quarter, step):
                ref.full[base + row : base + row + step, :] = chunk[row : row + step, :].astype(F32)
            row = ref.place[1] ^ (i % 2)
            found = 2 * (row % 2) + (stage_bit(row, stage) ^ flipped)
            middle = 4 * quarter - width
            for place in range(4):
                first, last = place * quarter, (place + 1) * quarter
                copies = []
                for j, (out, start, stop, offset) in enumerate(
                    (
                        (getattr(ref, f"inner_{i // 2}"), first, min(last, middle), 0),
                        (getattr(ref, f"outer_{i // 2}"), max(first, middle), last, middle),
                    )
                ):
                    if start < stop:
                        copies.append(
                            pltpu.make_async_copy(
                                ref.full.at[pl.ds(base + start - first, stop - start)],
                                out.at[pl.ds(start - offset, stop - start)],
                                ref.semaphores.at[2 * i + j],
                            )
                        )
                moves.append((found == place, copies))
            base += quarter
        for here, copies in moves:

            @pl.when(here)
            def _():
                for copy in copies:
                    copy.start()

        for here, copies in moves:
            pl.when(here)(lambda: wait_all(copies))

    return widen_sums


def held_back(arrays, place, before):
    keys = [f"array_{i}" for i in range(len(arrays))]

    @run_kernel(
        place,
        dict(before=before),
        {},
        {},
        renewed=dict(zip(keys, arrays.values())),
        work=0.01,
        memory=8,
    )
    def pass_on(ref):
        pass

    return {key: getattr(pass_on, name) for key, name in zip(arrays, keys)}


class RowSum:
    def __init__(self, keep, send, place, row):
        length = lax.axis_size("rows")
        bits = length.bit_length() - 1
        self.keep, self.send, self.place, self.row = keep, send, place, row
        self.half = keep.shape[0] - EXTRA
        self.direct = length == 1 << bits and (self.half >> (bits - 1)) % EXTRA == 0
        self.stages = [(0, 0), (1, 2), (2, 1)] + [(i, i) for i in range(3, bits)]
        if self.direct:
            self.received = exchange(send, self.stages[0])

    def halve(self, stage, *after):
        sent = add_part(self.keep, self.received, self.place, stage, 1, after)
        received = exchange(sent.sum_out, stage)
        self.keep = add_part(self.keep, self.received, self.place, stage, 0).sum_out
        self.received = received
        return sent.token

    def turn(self, *after):
        chunk = add_last(self.keep, self.received, self.place, after)
        self.own, self.extra = chunk.own_out, chunk.extra_out
        self.received = exchange(self.own, self.stages[-1])
        return chunk.token

    def double(self, stage, following, *after):
        joined = join(self.own, self.received, self.place, stage, after)
        self.own = joined.joined_out
        self.received = exchange(self.own, following)
        return joined.token

    def plain(self):
        width = self.keep.shape[1]
        even = self.row % 2 == 0
        pack = [jnp.where(even, self.keep, self.send)[: self.half]]
        pack.append(jnp.where(even, self.send, self.keep))
        total = lax.psum(jnp.concatenate(pack, axis=0), "rows").astype(F32)
        inner, outer, extra = jnp.split(total, (2 * self.half - width, 2 * self.half))
        return inner, outer, [extra[i : i + 1] for i in range(4)]


def sum_streams(streams, fillers):
    if not all(stream.direct for stream in streams):
        for filler in fillers:
            filler(())
        return [stream.plain() for stream in streams]
    stages = streams[0].stages
    mark = ()
    for i, stage in enumerate(stages[1:]):
        for stream in streams:
            mark = (stream.halve(stage, *mark),)
        if i == 2:
            mark = fillers[0](mark)
    for stream in streams[::-1]:
        mark = (stream.turn(*mark),)
    mark = fillers[1](mark)
    for stage, following in zip(stages[:1:-1], stages[-2:0:-1]):
        for stream in streams[::-1]:
            mark = (stream.double(stage, following, *mark),)
    place = streams[0].place
    extras = tuple(stream.extra for stream in streams)
    known = [(stream.own, exchange(stream.own, stages[0])) for stream in streams]
    first = unpack(known, place, stages[1], 0, None, extras)
    late = held_back({i: stream.received for i, stream in enumerate(streams)}, place, first.token)
    rest = [(late[i], exchange(late[i], stages[0])) for i in range(len(streams))]
    both = unpack(rest, place, stages[1], 1, first)
    return [
        (
            getattr(both, f"inner_{i}"),
            getattr(both, f"outer_{i}"),
            [getattr(first, f"line_{4 * i + j}") for j in range(4)],
        )
        for i in range(len(streams))
    ]


def per_device(
    node_latents,
    edge_latents,
    senders,
    receivers,
    cotangent,
    edge_weight_in,
    edge_bias_in,
    edge_weight_out,
    edge_bias_out,
    edge_gain,
    edge_shift,
    node_weight_in,
    node_bias_in,
    node_weight_out,
    node_bias_out,
    node_gain,
    node_shift,
):
    batches, count, width = node_latents.shape
    total = count * lax.axis_size("rows")
    row = lax.axis_index("rows")
    start = row * count
    place = jnp.stack([lax.axis_index("section"), row]).astype(jnp.int32)

    weights = dict(
        edge_in=edge_weight_in.reshape(3, width, width),
        edge_out=edge_weight_out[0],
        node_in=node_weight_in.reshape(2, width, width),
        node_out=node_weight_out[0],
    )
    vectors = (
        edge_bias_in,
        edge_bias_out,
        edge_gain,
        edge_shift,
        node_bias_in,
        node_bias_out,
        node_gain,
        node_shift,
    )
    swap = [(0, 1), (1, 0)]
    pieces = weight_pieces(weights, vectors, place)
    halo = neighbours(node_latents)
    near = dict(**weights, vectors_in=pieces.vectors_out)
    straight = lax.ppermute(pieces.own_out, "section", swap)
    crossed = lax.ppermute(pieces.other_out, "section", swap)
    third = lax.ppermute(pieces.third_out, "section", swap[1:])

    live = receivers >= 0
    targets = jnp.where(live, receivers - start, -1)
    sources = jnp.where(live, jnp.mod(senders - start + count, total), -1)
    positions = jnp.pad(jnp.stack([sources, targets], axis=1), ((0, 0), (0, 6), (0, 0)))

    near_run = layer_one(False, near, place, positions, halo, node_latents, edge_latents)
    near_low = near_run.states_low_out
    first = held_back({0: straight}, place, near_low)[0]
    near_halo = neighbours(near_low, 0)
    late = held_back(
        {2: within(first, lambda i: i ^ 2, 1), 3: third, 4: across(first, 4)}, place, near_halo
    )
    shared = {0: first, 6: crossed, 4: late[4]}
    for offset in list(shared):
        shared[offset ^ 1] = across(shared[offset], 1)
    fars = []
    for section, piece in enumerate((late[3], late[2])):
        found = {**shared, 2: piece, 3: within(piece, lambda i: i ^ 1, section)}
        fars.append(dict(far=tuple(found[offset] for offset in range(PIECES))))
    near_two = layer_two(
        False,
        fars[0],
        place,
        positions,
        near_halo,
        near_low,
        near_run.edges_out,
        cotangent,
    )
    after_near = dict(**fars[1], first=near_two.base_out)
    one = layer_one(True, after_near, place, positions, halo, node_latents, edge_latents)
    far_low = one.states_low_out
    far_two = layer_two(
        True,
        near,
        place,
        positions,
        neighbours(far_low, 1),
        far_low,
        one.edges_out,
        cotangent,
    )
    second = (near_two.base_out, *neighbours(near_two.to_pair_out, 0, near_two.to_other_out))
    back = layer_one_back(
        near,
        place,
        positions,
        halo,
        node_latents,
        edge_latents,
        near_run,
        near_two,
        far_two,
        second,
    )
    received = neighbours(back.to_pair_out, None, back.to_other_out)
    late = {}

    def finish_nodes(mark):
        late["nodes"] = node_outputs(
            place, near_run, far_two, back, received, mark
        )
        return (late["nodes"].token,)

    def finish_edges(mark):
        late["grads"], token = edge_outputs(
            near,
            place,
            near_two.edge_low_out,
            far_two.edge_low_out,
            back.hidden_out,
            mark,
        )
        return (token,)

    edge_sums, node_sums = sum_streams(
        [
            RowSum(back.edge_keep_out, back.edge_send_out, place, row),
            RowSum(back.node_keep_out, back.node_send_out, place, row),
        ],
        (finish_edges, finish_nodes),
    )
    lines = [line for sums in (edge_sums, node_sums) for line in sums[2]]
    return (
        late["nodes"].states_out.reshape(halo[0].shape)[None],
        late["nodes"].grads_out.reshape(halo[0].shape)[None],
        late["grads"].reshape(edge_latents.shape)[None],
        edge_sums[0][None],
        lines[0],
        edge_sums[1][None],
        *lines[1:4],
        node_sums[0][None],
        lines[4],
        node_sums[1][None],
        *lines[5:],
    )


def solution(mesh):
    batch_rows = P(None, "rows", None)
    matrix = P("section", None, None)
    vector = P("section", None)
    by_layer = P("section", None, "rows", None)
    weights = (matrix, vector, matrix, vector, vector, vector)
    in_specs = (batch_rows, batch_rows, P(None, "rows"), P(None, "rows"), batch_rows)
    return jax.shard_map(
        per_device,
        mesh=mesh,
        in_specs=in_specs + weights + weights,
        out_specs=(by_layer,) * 3 + weights + weights,
        check_vma=False,
    )
```

```python
from types import SimpleNamespace

import jax
import jax.numpy as jnp
from jax import lax
from jax.experimental import pallas as pl
from jax.experimental.pallas import tpu as pltpu
from jax.sharding import PartitionSpec as P

EPSILON = 1e-05
PIECES = 8
EXTRA = 16
TILE = 512
LANES = 128
MIB = 1024 * 1024
F32 = jnp.float32
LOW = jnp.bfloat16
EDGE_IN, SENDER_IN, TARGET_IN, EDGE_OUT, NODE_IN, SUMMED_IN, NODE_OUT = range(7)
MATRICES = 7
ORDER = (SENDER_IN, TARGET_IN, EDGE_IN, EDGE_OUT, NODE_IN, SUMMED_IN, NODE_OUT)


def dot_nn(left, right):
    return jnp.dot(left, right, preferred_element_type=F32)


def dot_nt(left, right):
    return lax.dot_general(left, right, (((1,), (1,)), ((), ())), preferred_element_type=F32)


def dot_tn(left, right):
    return lax.dot_general(left, right, (((0,), (0,)), ((), ())), preferred_element_type=F32)


def silu_parts(half):
    above = 1.0 + jnp.tanh(half)
    active = half * above
    return active, above + active * (2.0 - above)


def norm_parts(values):
    centred = values - jnp.mean(values, axis=-1, keepdims=True)
    scale = lax.rsqrt(jnp.mean(centred * centred, axis=-1, keepdims=True) + EPSILON)
    return centred * scale, scale


def norm_backward(scaled, unit, scale):
    first = jnp.mean(scaled, axis=-1, keepdims=True)
    second = jnp.mean(scaled * unit, axis=-1, keepdims=True)
    return scale * (scaled - first - unit * second)


def folded(values):
    rows, columns = values.shape
    return jnp.sum(values.reshape(rows // 8, 8, columns), axis=0)


def column_sum(values):
    return jnp.sum(values, axis=0, keepdims=True)


def hot_columns(index, width):
    places = lax.broadcasted_iota(jnp.int32, (index.shape[0], width), 1)
    return jnp.where(places == index, 1.0, 0.0).astype(LOW)


def hot_rows(index, height):
    places = lax.broadcasted_iota(jnp.int32, (height, index.shape[1]), 0)
    return jnp.where(places == index, 1.0, 0.0).astype(LOW)


def block(i, size):
    if isinstance(i, int):
        return pl.ds(i * size, size)
    return pl.ds(pl.multiple_of(i * size, size), size)


def repeat(count, body, looped):
    if not looped:
        for i in range(count):
            body(i)
        return

    def step(i, carry):
        body(i)
        return carry

    lax.fori_loop(0, count, step, 0)


def each_tile(batches, slots, body, looped):
    parts = slots // TILE

    def each_part(batch):
        for part in range(parts):
            body(batch, block(part, TILE), block(batch * parts + part, TILE))

    repeat(batches, each_part, looped)


class Copies:
    def __init__(self, semaphores):
        self.semaphores = semaphores
        self.used = 0
        self.leaving = []

    def semaphore(self):
        self.used += 1
        return self.semaphores.at[self.used - 1]

    def fetch(self, source, target):
        copy = pltpu.make_async_copy(source, target, self.semaphore())
        copy.start()
        return copy

    def fetch_either(self, flag, when_set, otherwise, target):
        semaphore = self.semaphore()
        copy = pltpu.make_async_copy(when_set, target, semaphore)
        other = pltpu.make_async_copy(otherwise, target, semaphore)
        pl.when(flag)(copy.start)
        pl.when(jnp.logical_not(flag))(other.start)
        return copy

    def send(self, source, target):
        self.leaving.append(self.fetch(source, target))

    def finish(self):
        wait_all(self.leaving)


def wait_all(copies):
    for copy in copies:
        copy.wait()


def run_kernel(
    place,
    inputs,
    outputs,
    scratch,
    near_inputs=None,
    near_outputs=None,
    renewed=None,
    work=1.0,
    memory=60,
    after=None,
    section=None,
):
    groups = []
    near_inputs = dict(near_inputs or {})
    near_outputs = dict(near_outputs or {})
    if after is not None:
        near_inputs.update(tokens=tuple(after))
        near_outputs.update(token=jax.ShapeDtypeStruct((8, LANES), F32))
    arguments = [place]
    in_specs = [pl.BlockSpec(memory_space=pltpu.SMEM)]
    far = pl.BlockSpec(memory_space=pl.ANY)
    close = pl.BlockSpec(memory_space=pltpu.VMEM)
    for group, spec in ((inputs, far), (near_inputs, close)):
        for key, value in group.items():
            items = value if isinstance(value, tuple) else (value,)
            groups.append((key, len(items), isinstance(value, tuple)))
            arguments += items
            in_specs += [spec] * len(items)
    renewed = renewed or {}
    shapes = {key: jax.ShapeDtypeStruct(item.shape, item.dtype) for key, item in renewed.items()}
    made = {**shapes, **outputs, **near_outputs}
    aliases = {len(arguments) + i: i for i in range(len(renewed))}
    first_old = len(arguments)
    arguments += renewed.values()
    in_specs += [far] * len(renewed)
    out_specs = [close if key in near_outputs else far for key in made]

    def decorate(body):
        def kernel(*refs):
            named = SimpleNamespace(place=refs[0])
            used = 1
            for key, size, several in groups:
                part = refs[used : used + size]
                setattr(named, key, part if several else part[0])
                used += size
            used = first_old + len(renewed)
            for key in (*made, *scratch):
                setattr(named, key, refs[used])
                used += 1
            if after is not None:
                named.token[...] = jnp.zeros_like(named.token)
            body(named)

        call = pl.pallas_call(
            kernel,
            out_shape=list(made.values()),
            in_specs=in_specs,
            out_specs=out_specs,
            input_output_aliases=aliases,
            scratch_shapes=list(scratch.values()),
            compiler_params=pltpu.CompilerParams(vmem_limit_bytes=memory * MIB),
            cost_estimate=pl.CostEstimate(
                flops=int(work * 4e9), bytes_accessed=int(work * 8e6), transcendentals=0
            ),
            name=body.__name__,
        )
        if section is None:
            results = call(*arguments)
        else:

            def nothing(*refs):
                pass

            skip = pl.pallas_call(
                nothing,
                out_shape=list(made.values()),
                in_specs=[],
                out_specs=out_specs,
                compiler_params=pltpu.CompilerParams(vmem_limit_bytes=memory * MIB),
            )
            here = lax.axis_index("section") == section
            results = lax.cond(here, call, lambda *unused: skip(), *arguments)
        return SimpleNamespace(**dict(zip(made, results)))

    return decorate


def shape(dims, kind=LOW):
    return jax.ShapeDtypeStruct(dims, kind)


def semaphores(count):
    return pltpu.SemaphoreType.DMA((count,))


def near_sources(ref):
    return [
        ref.edge_in.at[0],
        ref.edge_in.at[1],
        ref.edge_in.at[2],
        ref.edge_out,
        ref.node_in.at[0],
        ref.node_in.at[1],
        ref.node_out,
    ]


class Weights:
    def __init__(self, ref):
        self.target = ref.weights
        self.semaphores = ref.weight_semaphores

    def fetch_near(self, ref, order):
        sources = near_sources(ref)
        for matrix in order:
            pltpu.make_async_copy(
                sources[matrix], self.target.at[matrix], self.semaphores.at[matrix]
            ).start()

    def fetch_far(self, ref, order):
        piece = self.target.shape[1] // PIECES
        mine = ref.place[1] % PIECES
        for matrix in order:
            for offset, source in enumerate(ref.far):
                rows = pl.ds(pl.multiple_of((mine ^ offset) * piece, piece), piece)
                pltpu.make_async_copy(
                    source.at[pl.ds(matrix * piece, piece)],
                    self.target.at[matrix, rows],
                    self.semaphores.at[matrix],
                ).start()

    def wait(self, *order):
        for matrix in order:
            whole = self.target.at[matrix]
            pltpu.make_async_copy(whole, whole, self.semaphores.at[matrix]).wait()

    def __getitem__(self, matrix):
        return self.target[matrix]


def weight_scratch(width):
    return dict(
        weights=pltpu.VMEM((MATRICES, width, width), LOW),
        weight_semaphores=semaphores(MATRICES),
        vectors=pltpu.VMEM((EXTRA, width), LOW),
    )


def far_vectors(ref):
    return ref.far[0].at[pl.ds(ref.far[0].shape[0] - EXTRA, EXTRA)]


def project_nodes(spread, count, weights, vectors, joint):
    width = spread.shape[1]
    sender = 0.5 * dot_nn(spread, weights[SENDER_IN])
    middle = jnp.concatenate(
        [
            spread[start + count : start + 2 * count, :]
            for start in range(0, spread.shape[0], 3 * count)
        ],
        axis=0,
    )
    target = 0.5 * (dot_nn(middle, weights[TARGET_IN]) + vectors[0:1, :])
    half = weights[EDGE_IN] * 0.5
    for batch in range(spread.shape[0] // (3 * count)):
        joint[batch, :width, :] = half
        joint[batch, width : width + 3 * count, :] = sender[
            3 * count * batch : 3 * count * (batch + 1), :
        ].astype(LOW)
        joint[batch, width + 3 * count :, :] = target[
            count * batch : count * (batch + 1), :
        ].astype(LOW)
    return middle


def forward_tile(edges, hot_senders, hot_targets, joint, weights, vectors):
    joined = jnp.concatenate([edges, hot_senders, hot_targets], axis=1)
    active, slope = silu_parts(dot_nn(joined, joint))
    active = active.astype(LOW)
    unit, scale = norm_parts(dot_nn(active, weights[EDGE_OUT]) + vectors[1:2, :])
    return active, slope, unit, scale


def sum_updates(targets, units, vectors, count):
    hot = hot_rows(targets, count)
    degree = jnp.sum(hot.astype(F32), axis=1, keepdims=True)
    return vectors[2:3, :] * dot_nn(hot, units) + vectors[3:4, :] * degree


def node_forward(nodes, summed, weights, vectors):
    hidden = dot_nn(nodes, weights[NODE_IN]) + dot_nn(summed, weights[SUMMED_IN])
    active, slope = silu_parts(0.5 * (hidden + vectors[4:5, :]))
    active = active.astype(LOW)
    unit, scale = norm_parts(dot_nn(active, weights[NODE_OUT]) + vectors[5:6, :])
    states = nodes.astype(F32) + unit * vectors[6:7, :] + vectors[7:8, :]
    return states, active, slope, unit, scale


def node_backward(incoming, slope, unit, scale, weights, vectors):
    result_grad = norm_backward(incoming * vectors[6:7, :], unit, scale).astype(LOW)
    hidden_grad = (dot_nt(result_grad, weights[NODE_OUT]) * (0.5 * slope)).astype(LOW)
    base = incoming + dot_nt(hidden_grad, weights[NODE_IN])
    return result_grad, hidden_grad, base, dot_nt(hidden_grad, weights[SUMMED_IN])


def node_weight_grads(pack, nodes, summed, active, result_grad, hidden_grad, incoming, unit):
    width = nodes.shape[1]
    pack[:width, :] = dot_tn(nodes, hidden_grad).astype(LOW)
    pack[width : 2 * width, :] = dot_tn(summed, hidden_grad).astype(LOW)
    pack[2 * width : 3 * width, :] = dot_tn(active, result_grad).astype(LOW)
    sums = [
        column_sum(hidden_grad.astype(F32)),
        column_sum(result_grad.astype(F32)),
        column_sum(incoming * unit),
        column_sum(incoming),
    ]
    pack[3 * width :, :] = extra_rows(sums)


def extra_rows(sums):
    zeros = jnp.zeros((EXTRA - len(sums), sums[0].shape[1]), F32)
    return jnp.concatenate([*sums, zeros], axis=0).astype(LOW)


def backward_tile(incoming, slope, unit, scale, half_out, vectors):
    result_grad = norm_backward(incoming * vectors[2:3, :], unit, scale)
    low_grad = result_grad.astype(LOW)
    hidden_grad = (dot_nt(low_grad, half_out) * slope).astype(LOW)
    sums = (folded(result_grad), folded(incoming * unit), folded(incoming))
    return low_grad, hidden_grad, sums


def add_each(left, right):
    return tuple(a + b for a, b in zip(left, right))


def scattered(rows, hidden_grad, count):
    senders = dot_nn(hot_rows(rows[0:1, :], 3 * count), hidden_grad)
    targets = dot_nn(hot_rows(rows[1:2, :], count), hidden_grad)
    return senders, targets


def return_to_nodes(senders, targets, weights):
    count = targets.shape[0]
    grad = dot_nt(senders, weights[SENDER_IN])
    own = grad[count : 2 * count, :] + dot_nt(targets, weights[TARGET_IN])
    return grad[:count, :].astype(LOW), grad[2 * count :, :].astype(LOW), own


def send_pack(copies, row, pack, keep, send):
    half = (pack.shape[0] - EXTRA) // 2
    bit = row % 2
    for out, place in ((keep, bit), (send, 1 - bit)):
        rows = pl.ds(pl.multiple_of(place * half, half), half)
        copies.send(pack.at[rows], out.at[pl.ds(0, half)])
        copies.send(pack.at[pl.ds(2 * half, EXTRA)], out.at[pl.ds(half, EXTRA)])


def position_inputs(positions, halo, nodes, edges):
    return dict(rows=positions, spreads=(*halo, nodes), edges=edges)


def turned(rows):
    return jnp.transpose(rows.astype(F32)).astype(jnp.int32)


def spread_rows(ref, batch, count):
    odd = ref.place[1] % 2
    starts = ((3 * batch + 2 - 2 * odd) * count, (3 * batch + 2 * odd) * count)
    return [pl.ds(pl.multiple_of(start, count), count) for start in starts] + [
        pl.ds((3 * batch + 1) * count, count)
    ]


def fetch_spread(copies, ref, batches):
    count = ref.spreads[0].shape[1]
    return [
        copies.fetch(source.at[batch], ref.spread.at[rows])
        for batch in range(batches)
        for source, rows in zip(ref.spreads, spread_rows(ref, batch, count))
    ]


def by_parity(ref, below, above):
    odd = ref.place[1] % 2 == 1
    return jnp.where(odd, below, above), jnp.where(odd, above, below)


def layer_one(far, weights, place, positions, halo, nodes, edges):
    batches, count, width = nodes.shape
    slots = edges.shape[1]
    picked = batches
    chosen = range(batches)
    outputs = dict(
        states_low_out=shape((batches, count, width)), edges_out=shape((batches, slots, width))
    )
    if not far:
        outputs.update(
            states_out=shape((batches, count, width), F32),
            kept_out=shape((batches, 3, slots, width)),
            scales_out=shape((batches, slots, LANES), F32),
            node_kept_out=shape((batches, 3, count, width), F32),
            node_kept_low_out=shape((batches, 2, count, width)),
        )
    scratch = dict(
        **weight_scratch(width),
        joint=pltpu.VMEM((picked, 2 * width, width), LOW),
        spread=pltpu.VMEM((picked * 3 * count, width), LOW),
        edge_buffer=pltpu.VMEM((picked, slots, width), LOW),
        column_buffer=pltpu.VMEM((picked, slots, 8), jnp.int32),
        row_buffer=pltpu.VMEM((picked, 8, slots), jnp.int32),
        edges_new=pltpu.VMEM((picked, slots, width), LOW),
        summed=pltpu.VMEM((picked * count, width), LOW),
        states=pltpu.VMEM((picked, count, width), F32),
        states_low=pltpu.VMEM((picked, count, width), LOW),
        kept=pltpu.VMEM((picked, 3, slots, width), LOW),
        scales=pltpu.VMEM((picked, slots, LANES), F32),
        node_kept=pltpu.VMEM((picked, 3, count, width), F32),
        node_kept_low=pltpu.VMEM((picked, 2, count, width), LOW),
        semaphores=semaphores(48),
    )

    def work(ref):
        copies = Copies(ref.semaphores)
        weights = Weights(ref)
        first = [copies.fetch(far_vectors(ref) if far else ref.vectors_in, ref.vectors)]
        second = []
        first += fetch_spread(copies, ref, batches)
        fetch = weights.fetch_far if far else weights.fetch_near
        fetch(ref, ORDER[:3])
        for i, batch in enumerate(chosen):
            second.append(
                [
                    copies.fetch(ref.edges.at[batch], ref.edge_buffer.at[i]),
                    copies.fetch(ref.rows.at[batch], ref.row_buffer.at[i]),
                ]
            )
            if i == 0:
                fetch(ref, ORDER[3:])
        wait_all(first)
        vectors = ref.vectors[...].astype(F32)
        weights.wait(SENDER_IN, TARGET_IN, EDGE_IN)
        middle = project_nodes(ref.spread[...], count, weights, vectors, ref.joint)
        weights.wait(EDGE_OUT)
        for batch in range(batches):
            wait_all(second[batch])
            ref.column_buffer[batch] = turned(ref.row_buffer[batch])

        def edge_tile(batch, tile, _):
            index = ref.column_buffer[batch, tile, :]
            latents = ref.edge_buffer[batch, tile, :]
            active, slope, unit, scale = forward_tile(
                latents,
                hot_columns(index[:, 0:1], 3 * count),
                hot_columns(index[:, 1:2], count),
                ref.joint[batch],
                weights,
                vectors,
            )
            live = (index[:, 1:2] >= 0).astype(F32)
            update = (unit * vectors[2:3, :] + vectors[3:4, :]) * live
            ref.edges_new[batch, tile, :] = (latents.astype(F32) + update).astype(LOW)
            ref.kept[batch, 2, tile, :] = unit.astype(LOW)
            if not far:
                ref.kept[batch, 0, tile, :] = active
                ref.kept[batch, 1, tile, :] = slope.astype(LOW)
                ref.scales[batch, tile, :] = jnp.broadcast_to(scale, (TILE, LANES))

        def sum_batch(batch):
            targets = ref.row_buffer[batch, 1:2, :]
            summed = sum_updates(targets, ref.kept[batch, 2], vectors, count)
            ref.summed[block(batch, count), :] = summed.astype(LOW)

        if far:
            each_tile(batches, slots, edge_tile, True)
            repeat(batches, sum_batch, True)
        parts = slots // TILE
        for batch in range(batches):
            if not far:
                for part in range(parts):
                    edge_tile(batch, block(part, TILE), None)
            copies.send(ref.edges_new.at[batch], ref.edges_out.at[batch])
            if not far:
                copies.send(ref.kept.at[batch], ref.kept_out.at[batch])
                copies.send(ref.scales.at[batch], ref.scales_out.at[batch])
                sum_batch(batch)
        summed = ref.summed[...]
        weights.wait(NODE_IN, SUMMED_IN, NODE_OUT)
        states, active, slope, unit, scale = node_forward(middle, summed, weights, vectors)
        for i, batch in enumerate(chosen):
            rows = slice(i * count, (i + 1) * count)
            ref.states[i] = states[rows, :]
            ref.states_low[i] = states[rows, :].astype(LOW)
            copies.send(ref.states_low.at[i], ref.states_low_out.at[batch])
            if not far:
                copies.send(ref.states.at[i], ref.states_out.at[batch])
                ref.node_kept[i, 0] = slope[rows, :]
                ref.node_kept[i, 1] = unit[rows, :]
                ref.node_kept[i, 2] = jnp.broadcast_to(scale[rows, :], (count, width))
                ref.node_kept_low[i, 0] = summed[rows, :]
                ref.node_kept_low[i, 1] = active[rows, :]
                copies.send(ref.node_kept.at[i], ref.node_kept_out.at[batch])
                copies.send(ref.node_kept_low.at[i], ref.node_kept_low_out.at[batch])
        copies.finish()

    @run_kernel(
        place,
        dict(**weights, **position_inputs(positions, halo, nodes, edges)),
        outputs,
        scratch,
        section=1 if far else 0,
    )
    def layer_one_forward(ref):
        work(ref)

    return layer_one_forward


def layer_two(second, weights, place, positions, halo, nodes, edges, cotangent):
    batches, count, width = nodes.shape
    slots = edges.shape[1]
    every = batches * slots
    nodes_shape = (batches * count, width)
    outputs = dict(
        edge_low_out=shape((every, width)),
        base_out=shape(nodes_shape, F32),
        to_pair_out=shape(nodes_shape),
        to_other_out=shape(nodes_shape),
    )
    if second:
        outputs.update(
            states_out=shape(nodes_shape, F32),
            node_keep_out=shape((3 * width // 2 + EXTRA, width)),
            node_send_out=shape((3 * width // 2 + EXTRA, width)),
            edge_keep_out=shape((2 * width + EXTRA, width)),
            edge_send_out=shape((2 * width + EXTRA, width)),
        )
    all_low = pltpu.VMEM((every, width), LOW)
    scratch = dict(
        **weight_scratch(width),
        half_out=pltpu.VMEM((width, width), LOW),
        summed=pltpu.VMEM(nodes_shape, LOW),
        sums=pltpu.VMEM((3, 8, width), F32),
        senders=pltpu.VMEM((batches * 3 * count, width), LOW),
        targets=pltpu.VMEM(nodes_shape, F32),
        total=pltpu.VMEM((2, width, width), F32),
        joint=pltpu.VMEM((batches, 2 * width, width), LOW),
        spread=pltpu.VMEM((batches * 3 * count, width), LOW),
        edge_buffer=all_low,
        column_buffer=pltpu.VMEM((batches, slots, 8), jnp.int32),
        row_buffer=pltpu.VMEM((batches, 8, slots), jnp.int32),
        cotangent_buffer=pltpu.VMEM((batches * count, width), LOW),
        hot_targets=pltpu.VMEM((every, count), LOW),
        active_all=all_low,
        slope_all=all_low,
        unit_all=all_low,
        scales=pltpu.VMEM((every, LANES), F32),
        states=pltpu.VMEM(nodes_shape, F32),
        base=pltpu.VMEM(nodes_shape, F32),
        summed_grad=pltpu.VMEM(nodes_shape, LOW),
        result_grads=all_low,
        hidden_grads=all_low,
        edge_low=all_low,
        to_pair=pltpu.VMEM(nodes_shape, LOW),
        to_other=pltpu.VMEM(nodes_shape, LOW),
        node_pack=pltpu.VMEM((3 * width + EXTRA, width), LOW),
        edge_pack=pltpu.VMEM((4 * width + EXTRA, width), LOW),
        semaphores=semaphores(48),
    )
    inputs = dict(
        **weights, **position_inputs(positions, halo, nodes, edges), cotangent=cotangent
    )

    def work(ref):
        copies = Copies(ref.semaphores)
        weights = Weights(ref)
        first = [copies.fetch(ref.vectors_in if second else far_vectors(ref), ref.vectors)]
        first += fetch_spread(copies, ref, batches)
        fetch = weights.fetch_near if second else weights.fetch_far
        fetch(ref, ORDER[:3])
        loads = []
        for batch in range(batches):
            rows = pl.ds(batch * slots, slots)
            loads.append(
                [
                    copies.fetch(ref.edges.at[batch], ref.edge_buffer.at[rows]),
                    copies.fetch(ref.rows.at[batch], ref.row_buffer.at[batch]),
                ]
            )
            if batch == 0:
                fetch(ref, ORDER[3:])
        third = [
            copies.fetch(
                ref.cotangent.at[batch], ref.cotangent_buffer.at[pl.ds(batch * count, count)]
            )
            for batch in range(batches)
        ]
        wait_all(first)
        vectors = ref.vectors[...].astype(F32)
        weights.wait(SENDER_IN, TARGET_IN, EDGE_IN)
        middle = project_nodes(ref.spread[...], count, weights, vectors, ref.joint)
        weights.wait(EDGE_OUT)
        ref.half_out[...] = weights[EDGE_OUT] * 0.5
        for batch in range(batches):
            wait_all(loads[batch])
            ref.column_buffer[batch] = turned(ref.row_buffer[batch])

        def forward(batch, tile, place):
            index = ref.column_buffer[batch, tile, :]
            hot_targets = hot_columns(index[:, 1:2], count)
            active, slope, unit, scale = forward_tile(
                ref.edge_buffer[place, :],
                hot_columns(index[:, 0:1], 3 * count),
                hot_targets,
                ref.joint[batch],
                weights,
                vectors,
            )
            ref.hot_targets[place, :] = hot_targets
            if second:
                ref.active_all[place, :] = active
            ref.slope_all[place, :] = slope.astype(LOW)
            ref.unit_all[place, :] = unit.astype(LOW)
            ref.scales[place, :] = jnp.broadcast_to(scale, (TILE, LANES))

        def sum_batch(batch):
            units = ref.unit_all[block(batch, slots), :]
            targets = ref.row_buffer[batch, 1:2, :]
            summed = sum_updates(targets, units, vectors, count)
            ref.summed[block(batch, count), :] = summed.astype(LOW)

        each_tile(batches, slots, forward, second)
        repeat(batches, sum_batch, second)
        summed = ref.summed[...]
        wait_all(third)
        weights.wait(NODE_IN, SUMMED_IN, NODE_OUT)
        states, active, slope, unit, scale = node_forward(middle, summed, weights, vectors)
        ref.states[...] = states
        incoming = ref.cotangent_buffer[...].astype(F32)
        result_grad, hidden_grad, base, summed_grad = node_backward(
            incoming, slope, unit, scale, weights, vectors
        )
        ref.summed_grad[...] = summed_grad.astype(LOW)
        ref.base[...] = base
        if second:
            node_weight_grads(
                ref.node_pack, middle, summed, active, result_grad, hidden_grad, incoming, unit
            )
        if second:
            ref.sums[...] = jnp.zeros_like(ref.sums)

        def backward(batch, tile, place):
            incoming = dot_nn(
                ref.hot_targets[place, :], ref.summed_grad[block(batch, count), :]
            )
            low_grad, hidden_grad, more = backward_tile(
                incoming,
                ref.slope_all[place, :].astype(F32),
                ref.unit_all[place, :].astype(F32),
                jnp.concatenate([ref.scales[place, :]] * (width // LANES), axis=1),
                ref.half_out[...],
                vectors,
            )
            edge_grad = dot_nt(hidden_grad, weights[EDGE_IN])
            if second:
                for i, item in enumerate(more):
                    ref.sums[i] += item
                ref.result_grads[place, :] = low_grad
            ref.hidden_grads[place, :] = hidden_grad
            ref.edge_low[place, :] = edge_grad.astype(LOW)

        def scatter(batch):
            rows = block(batch, slots)
            here = block(batch, count)
            to_senders, to_targets = scattered(
                ref.row_buffer[batch], ref.hidden_grads[rows, :], count
            )
            to_senders = to_senders.astype(LOW)
            if second:
                ref.senders[block(batch, 3 * count), :] = to_senders
                ref.targets[here, :] = to_targets
            below, above, own = return_to_nodes(to_senders, to_targets.astype(LOW), weights)
            below, above = by_parity(ref, below, above)
            ref.to_pair[here, :] = below
            ref.to_other[here, :] = above
            ref.base[here, :] += own

        parts = slots // TILE
        if second:
            each_tile(batches, slots, backward, True)
            copies.send(ref.edge_low, ref.edge_low_out)
            repeat(batches, scatter, True)
        for batch in range(0 if second else batches):
            for part in range(parts):
                backward(batch, None, block(batch * parts + part, TILE))
            rows = block(batch, slots)
            copies.send(ref.edge_low.at[rows], ref.edge_low_out.at[rows])
            scatter(batch)
        copies.send(ref.to_pair, ref.to_pair_out)
        copies.send(ref.to_other, ref.to_other_out)
        copies.send(ref.base, ref.base_out)
        if second:
            copies.send(ref.states, ref.states_out)
            ref.total[...] = jnp.zeros_like(ref.total)

            def add_rows(i):
                rows = block(i, TILE)
                ref.total[0] += dot_tn(ref.edge_buffer[rows, :], ref.hidden_grads[rows, :])
                ref.total[1] += dot_tn(ref.active_all[rows, :], ref.result_grads[rows, :])

            repeat(every // TILE, add_rows, True)
            edge_weight_grads(
                ref.edge_pack,
                ref.total[0],
                ref.total[1],
                ref.spread[...],
                middle,
                ref.senders[...],
                ref.targets[...],
                [ref.sums[i] for i in range(3)],
            )
            send_pack(copies, ref.place[1], ref.edge_pack, ref.edge_keep_out, ref.edge_send_out)
            send_pack(copies, ref.place[1], ref.node_pack, ref.node_keep_out, ref.node_send_out)
        copies.finish()

    @run_kernel(place, inputs, outputs, scratch, work=6.0, section=1 if second else 0)
    def layer_two_both(ref):
        work(ref)

    return layer_two_both


def edge_weight_grads(pack, edge_part, active_part, spread, middle, senders, targets, sums):
    width = spread.shape[1]
    pack[:width, :] = edge_part.astype(LOW)
    pack[width : 2 * width, :] = dot_tn(spread, senders).astype(LOW)
    pack[2 * width : 3 * width, :] = dot_tn(middle, targets.astype(LOW)).astype(LOW)
    pack[3 * width : 4 * width, :] = active_part.astype(LOW)
    pack[4 * width :, :] = extra_rows([column_sum(targets), *map(column_sum, sums)])


def layer_one_back(weights, place, positions, halo, nodes, edges, near, two, packs, second):
    batches, count, width = nodes.shape
    slots = edges.shape[1]
    every = batches * slots
    nodes_shape = (batches * count, width)
    loaded = dict(
        base=second[0],
        from_pair=second[1],
        from_other=second[2],
        node_kept=near.node_kept_out,
        node_kept_low=near.node_kept_low_out,
    )
    outputs = dict(hidden_out=shape((every, width)))
    all_low = pltpu.VMEM((every, width), LOW)
    nodes_low = pltpu.VMEM(nodes_shape, LOW)
    scratch = dict(
        **weight_scratch(width),
        half_out=pltpu.VMEM((width, width), LOW),
        spread=pltpu.VMEM((batches * 3 * count, width), LOW),
        edge_buffer=all_low,
        column_buffer=pltpu.VMEM((batches, slots, 8), jnp.int32),
        row_buffer=pltpu.VMEM((batches, 8, slots), jnp.int32),
        kept=pltpu.VMEM((3, every, width), LOW),
        scales=pltpu.VMEM((every, LANES), F32),
        edge_low=all_low,
        summed_grad=nodes_low,
        to_pair=nodes_low,
        to_other=nodes_low,
        result_grads=all_low,
        hidden_grads=all_low,
        node_pack=pltpu.VMEM((3 * width + EXTRA, width), LOW),
        edge_pack=pltpu.VMEM((4 * width + EXTRA, width), LOW),
        semaphores=semaphores(64),
        **{key: pltpu.VMEM(value.shape, value.dtype) for key, value in loaded.items()},
    )
    renewed = dict(
        node_keep_out=packs.node_keep_out,
        node_send_out=packs.node_send_out,
        edge_keep_out=packs.edge_keep_out,
        edge_send_out=packs.edge_send_out,
        base_out=packs.base_out,
        to_pair_out=packs.to_pair_out,
        to_other_out=packs.to_other_out,
    )
    inputs = dict(
        **weights,
        **position_inputs(positions, halo, nodes, edges),
        loads=tuple(loaded.values()),
        edge_low_in=two.edge_low_out,
        scales_in=near.scales_out,
        kept_in=near.kept_out,
    )

    def stacked(items):
        return jnp.concatenate(items, axis=0)

    def work(ref):
        copies = Copies(ref.semaphores)
        weights = Weights(ref)
        first = [copies.fetch(ref.vectors_in, ref.vectors)]
        first += [copies.fetch(source, getattr(ref, key)) for key, source in zip(loaded, ref.loads)]
        weights.fetch_near(ref, (NODE_OUT, NODE_IN, SUMMED_IN))
        first += fetch_spread(copies, ref, batches)
        second = []
        third = []
        for batch in range(batches):
            rows = pl.ds(batch * slots, slots)
            second.append(
                [
                    copies.fetch(ref.edge_low_in.at[rows], ref.edge_low.at[rows]),
                    copies.fetch(ref.scales_in.at[batch], ref.scales.at[rows]),
                    copies.fetch(ref.kept_in.at[batch], ref.kept.at[:, rows]),
                    copies.fetch(ref.rows.at[batch], ref.row_buffer.at[batch]),
                ]
            )
            if batch == 0:
                weights.fetch_near(ref, (EDGE_OUT, SENDER_IN, TARGET_IN))
            third.append(copies.fetch(ref.edges.at[batch], ref.edge_buffer.at[rows]))
        wait_all(first)
        vectors = ref.vectors[...].astype(F32)
        weights.wait(NODE_OUT, NODE_IN, SUMMED_IN)
        middle = stacked(
            [
                ref.spread[(3 * batch + 1) * count : (3 * batch + 2) * count, :]
                for batch in range(batches)
            ]
        )
        incoming = (
            ref.base[...] + ref.from_pair[...].astype(F32) + ref.from_other[...].astype(F32)
        )
        incoming = incoming.astype(LOW).astype(F32)
        slope, unit, scale = (
            stacked([ref.node_kept[batch, i] for batch in range(batches)]) for i in range(3)
        )
        summed, active = (
            stacked([ref.node_kept_low[batch, i] for batch in range(batches)]) for i in range(2)
        )
        result_grad, hidden_grad, base, summed_grad = node_backward(
            incoming, slope, unit, scale, weights, vectors
        )
        ref.summed_grad[...] = summed_grad.astype(LOW)
        ref.base[...] = base
        node_weight_grads(
            ref.node_pack, middle, summed, active, result_grad, hidden_grad, incoming, unit
        )
        weights.wait(EDGE_OUT, SENDER_IN, TARGET_IN)
        ref.half_out[...] = weights[EDGE_OUT] * 0.5
        sums = None
        senders = []
        targets = []
        for batch in range(batches):
            wait_all(second[batch])
            ref.column_buffer[batch] = turned(ref.row_buffer[batch])
            nodes_here = slice(batch * count, (batch + 1) * count)
            for part in range(slots // TILE):
                tile, place = block(part, TILE), block(batch * (slots // TILE) + part, TILE)
                hot = hot_columns(ref.column_buffer[batch, tile, 1:2], count)
                incoming = ref.edge_low[place, :].astype(F32) + dot_nn(
                    hot, ref.summed_grad[nodes_here, :]
                )
                low_grad, hidden_grad, more = backward_tile(
                    incoming,
                    ref.kept[1, place, :].astype(F32),
                    ref.kept[2, place, :].astype(F32),
                    jnp.concatenate([ref.scales[place, :]] * (width // LANES), axis=1),
                    ref.half_out[...],
                    vectors,
                )
                sums = more if sums is None else add_each(sums, more)
                ref.result_grads[place, :] = low_grad
                ref.hidden_grads[place, :] = hidden_grad
            rows = slice(batch * slots, (batch + 1) * slots)
            to_senders, to_targets = scattered(
                ref.row_buffer[batch], ref.hidden_grads[rows, :], count
            )
            senders.append(to_senders.astype(LOW))
            targets.append(to_targets)
        wait_all(third)
        copies.send(ref.hidden_grads, ref.hidden_out)
        edge_weight_grads(
            ref.edge_pack,
            dot_tn(ref.edge_buffer[...], ref.hidden_grads[...]),
            dot_tn(ref.kept[0], ref.result_grads[...]),
            ref.spread[...],
            middle,
            stacked(senders),
            stacked(targets),
            sums,
        )
        send_pack(copies, ref.place[1], ref.edge_pack, ref.edge_keep_out, ref.edge_send_out)
        send_pack(copies, ref.place[1], ref.node_pack, ref.node_keep_out, ref.node_send_out)
        for batch in range(batches):
            nodes_here = slice(batch * count, (batch + 1) * count)
            below, above, own = return_to_nodes(
                senders[batch], targets[batch].astype(LOW), weights
            )
            below, above = by_parity(ref, below, above)
            ref.to_pair[nodes_here, :] = below
            ref.to_other[nodes_here, :] = above
            ref.base[nodes_here, :] += own
        copies.send(ref.to_pair, ref.to_pair_out)
        copies.send(ref.to_other, ref.to_other_out)
        copies.send(ref.base, ref.base_out)
        copies.finish()

    @run_kernel(place, inputs, outputs, scratch, renewed=renewed, work=6.0)
    def layer_one_backward(ref):
        pl.when(ref.place[0] == 0)(lambda: work(ref))

    return layer_one_backward


def edge_outputs(weights, place, near_low, far_low, hidden, after):
    every, width = near_low.shape
    scratch = dict(
        edge_weight=pltpu.VMEM((width, width), LOW),
        edge_buffer=pltpu.VMEM((every, width), LOW),
        hidden_buffer=pltpu.VMEM((every, width), LOW),
        full=pltpu.VMEM((every, width), F32),
        semaphores=semaphores(2 * every // TILE + every // TILE + 1),
    )

    @run_kernel(
        place,
        dict(
            edge_in=weights["edge_in"],
            near_low=near_low,
            far_low=far_low,
            hidden=hidden,
        ),
        dict(edge_grads_out=shape((every, width), F32)),
        scratch,
        work=0.05,
        after=after,
    )
    def edge_gradients(ref):
        first_section = ref.place[0] == 0
        copies = Copies(ref.semaphores)
        weight = copies.fetch(ref.edge_in.at[0], ref.edge_weight)
        arriving = [
            [
                copies.fetch(ref.hidden.at[tile], ref.hidden_buffer.at[tile]),
                copies.fetch_either(
                    first_section,
                    ref.near_low.at[tile],
                    ref.far_low.at[tile],
                    ref.edge_buffer.at[tile],
                ),
            ]
            for tile in [block(i, TILE) for i in range(every // TILE)]
        ]
        weight.wait()
        for tile, loads in zip([block(i, TILE) for i in range(every // TILE)], arriving):
            wait_all(loads)
            edge_in = ref.edge_buffer[tile, :].astype(F32)

            @pl.when(ref.place[0] == 0)
            def _():
                more = dot_nt(ref.hidden_buffer[tile, :], ref.edge_weight[...])
                ref.full[tile, :] = edge_in + more

            @pl.when(ref.place[0] == 1)
            def _():
                ref.full[tile, :] = edge_in

            copies.send(ref.full.at[tile], ref.edge_grads_out.at[tile])
        copies.finish()

    return edge_gradients.edge_grads_out, edge_gradients.token


def node_outputs(place, near, far_two, back, received, after):
    dims = far_two.states_out.shape
    full = pltpu.VMEM(dims, F32)
    low = pltpu.VMEM(dims, LOW)

    @run_kernel(
        place,
        dict(
            parts=(back.base_out, *received),
            near=near.states_out.reshape(dims),
            far=far_two.states_out,
        ),
        dict(grads_out=shape(dims, F32), states_out=shape(dims, F32)),
        dict(base=full, below=low, above=low, states=full, semaphores=semaphores(6)),
        work=0.02,
        after=after,
    )
    def finish_nodes(ref):
        first_section = ref.place[0] == 0
        copies = Copies(ref.semaphores)
        states = copies.fetch_either(first_section, ref.near, ref.far, ref.states)
        wait_all(
            [copies.fetch(*pair) for pair in zip(ref.parts, (ref.base, ref.below, ref.above))]
        )
        total = ref.base[...] + ref.below[...].astype(F32) + ref.above[...].astype(F32)
        ref.base[...] = jnp.where(first_section, total, total.astype(LOW).astype(F32))
        copies.send(ref.base, ref.grads_out)
        states.wait()
        copies.send(ref.states, ref.states_out)
        copies.finish()

    return finish_nodes


def weight_pieces(weights, vectors, place):
    width = weights["edge_out"].shape[1]
    piece = width // PIECES
    rows = MATRICES * piece + EXTRA

    @run_kernel(
        place,
        dict(**weights, lines=vectors),
        dict(
            own_out=shape((rows, width)),
            other_out=shape((rows, width)),
            vectors_out=shape((EXTRA, width)),
        ),
        dict(
            own=pltpu.VMEM((rows, width), LOW),
            other=pltpu.VMEM((rows, width), LOW),
            single=pltpu.VMEM((len(vectors), 1, width), LOW),
            semaphores=semaphores(2 * MATRICES + len(vectors) + 3),
        ),
        work=0.02,
    )
    def weight_piece(ref):
        copies = Copies(ref.semaphores)
        mine = ref.place[1] % PIECES
        sources = near_sources(ref)
        lines = [copies.fetch(line, ref.single.at[i]) for i, line in enumerate(ref.lines)]
        arriving = []
        for buffer, offset in ((ref.own, 0), (ref.other, 6)):
            place = pl.ds(pl.multiple_of((mine ^ offset) * piece, piece), piece)
            for matrix, source in enumerate(sources):
                target = buffer.at[pl.ds(matrix * piece, piece)]
                arriving.append(copies.fetch(source.at[place], target))
        wait_all(lines)
        extra = extra_rows([ref.single[i].astype(F32) for i in range(len(lines))])
        for buffer in (ref.own, ref.other):
            buffer[MATRICES * piece :, :] = extra
        wait_all(arriving)
        copies.send(ref.own, ref.own_out)
        copies.send(ref.other, ref.other_out)
        copies.send(ref.own.at[pl.ds(MATRICES * piece, EXTRA)], ref.vectors_out)
        copies.finish()

    return weight_piece


def along_rows(value, route):
    length = lax.axis_size("rows")
    return lax.ppermute(value, "rows", [(i, route(i)) for i in range(length)])


def neighbours(value, section=None, other=None):
    length = lax.axis_size("rows")
    pair = [(i, i ^ 1) for i in range(length)]
    beside = [(i, (i + 1 if i % 2 else i - 1) % length) for i in range(length)]
    axes = "rows"
    if section is not None:
        axes = ("section", "rows")
        start = section * length
        pair, beside = (
            [(start + one, start + two) for one, two in pairs] for pairs in (pair, beside)
        )
    return (
        lax.ppermute(value, axes, pair),
        lax.ppermute(value if other is None else other, axes, beside),
    )


def across(value, mask):
    return along_rows(value, lambda i: i ^ mask)


def exchange(value, stage):
    return along_rows(value, lambda i: i ^ (1 << stage[i % 2]))


def stage_bit(row, stage):
    return (row >> jnp.where(row % 2 == 0, stage[0], stage[1])) & 1


def add_part(kept, received, place, stage, other, after=None):
    rows, width = kept.shape
    half = (rows - EXTRA) // 2

    @run_kernel(
        place,
        {},
        {},
        {},
        near_inputs=dict(kept=kept, received=received),
        near_outputs=dict(sum_out=shape((half + EXTRA, width))),
        work=0.01,
        memory=8,
        after=after,
    )
    def add_halves(ref):
        bit = stage_bit(ref.place[1], stage)
        part = pl.ds(pl.multiple_of((1 - bit if other else bit) * half, EXTRA), half)
        total = ref.kept[part, :].astype(F32) + ref.received[part, :].astype(F32)
        ref.sum_out[:half, :] = total.astype(LOW)
        total = ref.kept[2 * half :, :].astype(F32) + ref.received[2 * half :, :].astype(F32)
        ref.sum_out[half:, :] = total.astype(LOW)

    return add_halves


def add_last(kept, received, place, after):
    rows, width = kept.shape
    rows = rows - EXTRA

    @run_kernel(
        place,
        {},
        {},
        {},
        near_inputs=dict(kept=kept, received=received),
        near_outputs=dict(own_out=shape((rows, width)), extra_out=shape((EXTRA, width), F32)),
        work=0.01,
        memory=8,
        after=after,
    )
    def add_chunk(ref):
        total = ref.kept[...].astype(F32) + ref.received[...].astype(F32)
        ref.own_out[...] = total[:rows, :].astype(LOW)
        ref.extra_out[...] = total[rows:, :]

    return add_chunk


def join(own, received, place, stage, after):
    rows, width = own.shape

    @run_kernel(
        place,
        {},
        {},
        {},
        near_inputs=dict(own=own, received=received),
        near_outputs=dict(joined_out=shape((2 * rows, width))),
        work=0.01,
        memory=8,
        after=after,
    )
    def join_halves(ref):
        bit = stage_bit(ref.place[1], stage)
        for source, side in ((ref.own, bit), (ref.received, 1 - bit)):
            ref.joined_out[pl.ds(pl.multiple_of(side * rows, EXTRA), rows), :] = source[...]

    return join_halves


def unpack(pairs, place, stage, flipped, previous, extras=()):
    width = pairs[0][0].shape[1]
    quarters = [pair[0].shape[0] for pair in pairs]
    renewed = {}
    outputs = {}
    for i, quarter in enumerate(quarters):
        outputs[f"inner_{i}"] = shape((4 * quarter - width, width), F32)
        outputs[f"outer_{i}"] = shape((width, width), F32)
    if previous is not None:
        renewed = {key: getattr(previous, key) for key in outputs}
        outputs = {}
    lines = {f"line_{i}": shape((1, width), F32) for i in range(4 * len(extras))}
    chunks = tuple(chunk for pair in pairs for chunk in pair)

    @run_kernel(
        place,
        {},
        outputs,
        dict(
            full=pltpu.VMEM((2 * sum(quarters), width), F32),
            semaphores=semaphores(4 * len(pairs)),
        ),
        near_inputs=dict(chunks=chunks, extras=extras),
        near_outputs=lines,
        renewed=renewed,
        work=0.02,
        memory=16,
        after=(),
    )
    def widen_sums(ref):
        for i in range(len(lines)):
            getattr(ref, f"line_{i}")[...] = ref.extras[i // 4][i % 4 : i % 4 + 1, :]
        step = EXTRA * 8
        moves = []
        base = 0
        for i, chunk in enumerate(ref.chunks):
            quarter = chunk.shape[0]
            for row in range(0, quarter, step):
                ref.full[base + row : base + row + step, :] = chunk[row : row + step, :].astype(F32)
            row = ref.place[1] ^ (i % 2)
            found = 2 * (row % 2) + (stage_bit(row, stage) ^ flipped)
            middle = 4 * quarter - width
            for place in range(4):
                first, last = place * quarter, (place + 1) * quarter
                copies = []
                for j, (out, start, stop, offset) in enumerate(
                    (
                        (getattr(ref, f"inner_{i // 2}"), first, min(last, middle), 0),
                        (getattr(ref, f"outer_{i // 2}"), max(first, middle), last, middle),
                    )
                ):
                    if start < stop:
                        copies.append(
                            pltpu.make_async_copy(
                                ref.full.at[pl.ds(base + start - first, stop - start)],
                                out.at[pl.ds(start - offset, stop - start)],
                                ref.semaphores.at[2 * i + j],
                            )
                        )
                moves.append((found == place, copies))
            base += quarter
        for here, copies in moves:

            @pl.when(here)
            def _():
                for copy in copies:
                    copy.start()

        for here, copies in moves:
            pl.when(here)(lambda: wait_all(copies))

    return widen_sums


def held_back(arrays, place, before):
    keys = [f"array_{i}" for i in range(len(arrays))]

    @run_kernel(
        place,
        dict(before=before),
        {},
        {},
        renewed=dict(zip(keys, arrays.values())),
        work=0.01,
        memory=8,
    )
    def pass_on(ref):
        pass

    return {key: getattr(pass_on, name) for key, name in zip(arrays, keys)}


class RowSum:
    def __init__(self, keep, send, place, row):
        length = lax.axis_size("rows")
        bits = length.bit_length() - 1
        self.keep, self.send, self.place, self.row = keep, send, place, row
        self.half = keep.shape[0] - EXTRA
        self.direct = length == 1 << bits and (self.half >> (bits - 1)) % EXTRA == 0
        self.stages = [(0, 0), (1, 2), (2, 1)] + [(i, i) for i in range(3, bits)]
        if self.direct:
            self.received = exchange(send, self.stages[0])

    def halve(self, stage, *after):
        sent = add_part(self.keep, self.received, self.place, stage, 1, after)
        received = exchange(sent.sum_out, stage)
        self.keep = add_part(self.keep, self.received, self.place, stage, 0).sum_out
        self.received = received
        return sent.token

    def turn(self, *after):
        chunk = add_last(self.keep, self.received, self.place, after)
        self.own, self.extra = chunk.own_out, chunk.extra_out
        self.received = exchange(self.own, self.stages[-1])
        return chunk.token

    def double(self, stage, following, *after):
        joined = join(self.own, self.received, self.place, stage, after)
        self.own = joined.joined_out
        self.received = exchange(self.own, following)
        return joined.token

    def plain(self):
        width = self.keep.shape[1]
        even = self.row % 2 == 0
        pack = [jnp.where(even, self.keep, self.send)[: self.half]]
        pack.append(jnp.where(even, self.send, self.keep))
        total = lax.psum(jnp.concatenate(pack, axis=0), "rows").astype(F32)
        inner, outer, extra = jnp.split(total, (2 * self.half - width, 2 * self.half))
        return inner, outer, [extra[i : i + 1] for i in range(4)]


def sum_streams(streams, fillers):
    if not all(stream.direct for stream in streams):
        for filler in fillers:
            filler(())
        return [stream.plain() for stream in streams]
    stages = streams[0].stages
    mark = ()
    for i, stage in enumerate(stages[1:]):
        for stream in streams:
            mark = (stream.halve(stage, *mark),)
        if i == 2:
            mark = fillers[0](mark)
    for stream in streams[::-1]:
        mark = (stream.turn(*mark),)
    mark = fillers[1](mark)
    for stage, following in zip(stages[:1:-1], stages[-2:0:-1]):
        for stream in streams[::-1]:
            mark = (stream.double(stage, following, *mark),)
    place = streams[0].place
    extras = tuple(stream.extra for stream in streams)
    known = [(stream.own, exchange(stream.own, stages[0])) for stream in streams]
    first = unpack(known, place, stages[1], 0, None, extras)
    late = held_back({i: stream.received for i, stream in enumerate(streams)}, place, first.token)
    rest = [(late[i], exchange(late[i], stages[0])) for i in range(len(streams))]
    both = unpack(rest, place, stages[1], 1, first)
    return [
        (
            getattr(both, f"inner_{i}"),
            getattr(both, f"outer_{i}"),
            [getattr(first, f"line_{4 * i + j}") for j in range(4)],
        )
        for i in range(len(streams))
    ]


def per_device(
    node_latents,
    edge_latents,
    senders,
    receivers,
    cotangent,
    edge_weight_in,
    edge_bias_in,
    edge_weight_out,
    edge_bias_out,
    edge_gain,
    edge_shift,
    node_weight_in,
    node_bias_in,
    node_weight_out,
    node_bias_out,
    node_gain,
    node_shift,
):
    batches, count, width = node_latents.shape
    total = count * lax.axis_size("rows")
    row = lax.axis_index("rows")
    start = row * count
    place = jnp.stack([lax.axis_index("section"), row]).astype(jnp.int32)

    weights = dict(
        edge_in=edge_weight_in.reshape(3, width, width),
        edge_out=edge_weight_out[0],
        node_in=node_weight_in.reshape(2, width, width),
        node_out=node_weight_out[0],
    )
    vectors = (
        edge_bias_in,
        edge_bias_out,
        edge_gain,
        edge_shift,
        node_bias_in,
        node_bias_out,
        node_gain,
        node_shift,
    )
    swap = [(0, 1), (1, 0)]
    pieces = weight_pieces(weights, vectors, place)
    halo = neighbours(node_latents)
    near = dict(**weights, vectors_in=pieces.vectors_out)
    straight = lax.ppermute(pieces.own_out, "section", swap)
    crossed = lax.ppermute(pieces.other_out, "section", swap)

    live = receivers >= 0
    targets = jnp.where(live, receivers - start, -1)
    sources = jnp.where(live, jnp.mod(senders - start + count, total), -1)
    positions = jnp.pad(jnp.stack([sources, targets], axis=1), ((0, 0), (0, 6), (0, 0)))

    near_run = layer_one(False, near, place, positions, halo, node_latents, edge_latents)
    near_low = near_run.states_low_out
    first = held_back({0: straight}, place, near_low)[0]
    found = {0: first, 6: crossed, 2: across(first, 2), 4: across(first, 4)}
    near_halo = neighbours(near_low, 0)
    found.update(held_back({key: found[key] for key in (2, 4)}, place, near_halo))
    for offset in list(found):
        found[offset ^ 1] = across(found[offset], 1)
    far = dict(far=tuple(found[offset] for offset in range(PIECES)))
    near_two = layer_two(
        False,
        far,
        place,
        positions,
        near_halo,
        near_low,
        near_run.edges_out,
        cotangent,
    )
    after_near = dict(**far, first=near_two.base_out)
    one = layer_one(True, after_near, place, positions, halo, node_latents, edge_latents)
    far_low = one.states_low_out
    far_two = layer_two(
        True,
        near,
        place,
        positions,
        neighbours(far_low, 1),
        far_low,
        one.edges_out,
        cotangent,
    )
    second = (near_two.base_out, *neighbours(near_two.to_pair_out, 0, near_two.to_other_out))
    back = layer_one_back(
        near,
        place,
        positions,
        halo,
        node_latents,
        edge_latents,
        near_run,
        near_two,
        far_two,
        second,
    )
    received = neighbours(back.to_pair_out, None, back.to_other_out)
    late = {}

    def finish_nodes(mark):
        late["nodes"] = node_outputs(
            place, near_run, far_two, back, received, mark
        )
        return (late["nodes"].token,)

    def finish_edges(mark):
        late["grads"], token = edge_outputs(
            near,
            place,
            near_two.edge_low_out,
            far_two.edge_low_out,
            back.hidden_out,
            mark,
        )
        return (token,)

    edge_sums, node_sums = sum_streams(
        [
            RowSum(back.edge_keep_out, back.edge_send_out, place, row),
            RowSum(back.node_keep_out, back.node_send_out, place, row),
        ],
        (finish_edges, finish_nodes),
    )
    lines = [line for sums in (edge_sums, node_sums) for line in sums[2]]
    return (
        late["nodes"].states_out.reshape(halo[0].shape)[None],
        late["nodes"].grads_out.reshape(halo[0].shape)[None],
        late["grads"].reshape(edge_latents.shape)[None],
        edge_sums[0][None],
        lines[0],
        edge_sums[1][None],
        *lines[1:4],
        node_sums[0][None],
        lines[4],
        node_sums[1][None],
        *lines[5:],
    )


def solution(mesh):
    batch_rows = P(None, "rows", None)
    matrix = P("section", None, None)
    vector = P("section", None)
    by_layer = P("section", None, "rows", None)
    weights = (matrix, vector, matrix, vector, vector, vector)
    in_specs = (batch_rows, batch_rows, P(None, "rows"), P(None, "rows"), batch_rows)
    return jax.shard_map(
        per_device,
        mesh=mesh,
        in_specs=in_specs + weights + weights,
        out_specs=(by_layer,) * 3 + weights + weights,
        check_vma=False,
    )
```

```python
from types import SimpleNamespace

import jax
import jax.numpy as jnp
from jax import lax
from jax.experimental import pallas as pl
from jax.experimental.pallas import tpu as pltpu
from jax.sharding import PartitionSpec as P

EPSILON = 1e-05
PIECES = 8
EXTRA = 16
TILE = 512
LANES = 128
MIB = 1024 * 1024
F32 = jnp.float32
LOW = jnp.bfloat16
EDGE_IN, SENDER_IN, TARGET_IN, EDGE_OUT, NODE_IN, SUMMED_IN, NODE_OUT = range(7)
MATRICES = 7
ORDER = (SENDER_IN, TARGET_IN, EDGE_IN, EDGE_OUT, NODE_IN, SUMMED_IN, NODE_OUT)


def dot_nn(left, right):
    return jnp.dot(left, right, preferred_element_type=F32)


def dot_nt(left, right):
    return lax.dot_general(left, right, (((1,), (1,)), ((), ())), preferred_element_type=F32)


def dot_tn(left, right):
    return lax.dot_general(left, right, (((0,), (0,)), ((), ())), preferred_element_type=F32)


def silu_parts(half):
    above = 1.0 + jnp.tanh(half)
    active = half * above
    return active, above + active * (2.0 - above)


def norm_parts(values):
    centred = values - jnp.mean(values, axis=-1, keepdims=True)
    scale = lax.rsqrt(jnp.mean(centred * centred, axis=-1, keepdims=True) + EPSILON)
    return centred * scale, scale


def norm_backward(scaled, unit, scale):
    first = jnp.mean(scaled, axis=-1, keepdims=True)
    second = jnp.mean(scaled * unit, axis=-1, keepdims=True)
    return scale * (scaled - first - unit * second)


def folded(values):
    rows, columns = values.shape
    return jnp.sum(values.reshape(rows // 8, 8, columns), axis=0)


def column_sum(values):
    return jnp.sum(values, axis=0, keepdims=True)


def hot_columns(index, width):
    places = lax.broadcasted_iota(jnp.int32, (index.shape[0], width), 1)
    return jnp.where(places == index, 1.0, 0.0).astype(LOW)


def hot_rows(index, height):
    places = lax.broadcasted_iota(jnp.int32, (height, index.shape[1]), 0)
    return jnp.where(places == index, 1.0, 0.0).astype(LOW)


def block(i, size):
    if isinstance(i, int):
        return pl.ds(i * size, size)
    return pl.ds(pl.multiple_of(i * size, size), size)


def repeat(count, body, looped):
    if not looped:
        for i in range(count):
            body(i)
        return

    def step(i, carry):
        body(i)
        return carry

    lax.fori_loop(0, count, step, 0)


def each_tile(batches, slots, body, looped):
    parts = slots // TILE
    if looped == 2:
        repeat(
            batches * parts,
            lambda i: body(i // parts, block(i % parts, TILE), block(i, TILE)),
            True,
        )
        return

    def each_part(batch):
        for part in range(parts):
            body(batch, block(part, TILE), block(batch * parts + part, TILE))

    repeat(batches, each_part, looped)


class Copies:
    def __init__(self, semaphores):
        self.semaphores = semaphores
        self.used = 0
        self.leaving = []

    def semaphore(self):
        self.used += 1
        return self.semaphores.at[self.used - 1]

    def fetch(self, source, target):
        copy = pltpu.make_async_copy(source, target, self.semaphore())
        copy.start()
        return copy

    def fetch_either(self, flag, when_set, otherwise, target):
        semaphore = self.semaphore()
        copy = pltpu.make_async_copy(when_set, target, semaphore)
        other = pltpu.make_async_copy(otherwise, target, semaphore)
        pl.when(flag)(copy.start)
        pl.when(jnp.logical_not(flag))(other.start)
        return copy

    def send(self, source, target):
        self.leaving.append(self.fetch(source, target))

    def finish(self):
        wait_all(self.leaving)


def wait_all(copies):
    for copy in copies:
        copy.wait()


def run_kernel(
    place,
    inputs,
    outputs,
    scratch,
    near_inputs=None,
    near_outputs=None,
    renewed=None,
    work=1.0,
    memory=60,
    after=None,
    section=None,
):
    groups = []
    near_inputs = dict(near_inputs or {})
    near_outputs = dict(near_outputs or {})
    if after is not None:
        near_inputs.update(tokens=tuple(after))
        near_outputs.update(token=jax.ShapeDtypeStruct((8, LANES), F32))
    arguments = [place]
    in_specs = [pl.BlockSpec(memory_space=pltpu.SMEM)]
    far = pl.BlockSpec(memory_space=pl.ANY)
    close = pl.BlockSpec(memory_space=pltpu.VMEM)
    for group, spec in ((inputs, far), (near_inputs, close)):
        for key, value in group.items():
            items = value if isinstance(value, tuple) else (value,)
            groups.append((key, len(items), isinstance(value, tuple)))
            arguments += items
            in_specs += [spec] * len(items)
    renewed = renewed or {}
    shapes = {key: jax.ShapeDtypeStruct(item.shape, item.dtype) for key, item in renewed.items()}
    made = {**shapes, **outputs, **near_outputs}
    aliases = {len(arguments) + i: i for i in range(len(renewed))}
    first_old = len(arguments)
    arguments += renewed.values()
    in_specs += [far] * len(renewed)
    out_specs = [close if key in near_outputs else far for key in made]

    def decorate(body):
        def kernel(*refs):
            named = SimpleNamespace(place=refs[0])
            used = 1
            for key, size, several in groups:
                part = refs[used : used + size]
                setattr(named, key, part if several else part[0])
                used += size
            used = first_old + len(renewed)
            for key in (*made, *scratch):
                setattr(named, key, refs[used])
                used += 1
            if after is not None:
                named.token[...] = jnp.zeros_like(named.token)
            body(named)

        call = pl.pallas_call(
            kernel,
            out_shape=list(made.values()),
            in_specs=in_specs,
            out_specs=out_specs,
            input_output_aliases=aliases,
            scratch_shapes=list(scratch.values()),
            compiler_params=pltpu.CompilerParams(vmem_limit_bytes=memory * MIB),
            cost_estimate=pl.CostEstimate(
                flops=int(work * 4e9), bytes_accessed=int(work * 8e6), transcendentals=0
            ),
            name=body.__name__,
        )
        if section is None:
            results = call(*arguments)
        else:

            def nothing(*refs):
                pass

            skip = pl.pallas_call(
                nothing,
                out_shape=list(made.values()),
                in_specs=[],
                out_specs=out_specs,
                compiler_params=pltpu.CompilerParams(vmem_limit_bytes=memory * MIB),
            )
            here = lax.axis_index("section") == section
            results = lax.cond(here, call, lambda *unused: skip(), *arguments)
        return SimpleNamespace(**dict(zip(made, results)))

    return decorate


def shape(dims, kind=LOW):
    return jax.ShapeDtypeStruct(dims, kind)


def semaphores(count):
    return pltpu.SemaphoreType.DMA((count,))


def near_sources(ref):
    return [
        ref.edge_in.at[0],
        ref.edge_in.at[1],
        ref.edge_in.at[2],
        ref.edge_out,
        ref.node_in.at[0],
        ref.node_in.at[1],
        ref.node_out,
    ]


class Weights:
    def __init__(self, ref):
        self.target = ref.weights
        self.semaphores = ref.weight_semaphores

    def fetch_near(self, ref, order):
        sources = near_sources(ref)
        for matrix in order:
            pltpu.make_async_copy(
                sources[matrix], self.target.at[matrix], self.semaphores.at[matrix]
            ).start()

    def fetch_far(self, ref, order):
        piece = self.target.shape[1] // PIECES
        mine = ref.place[1] % PIECES
        for matrix in order:
            for offset, source in enumerate(ref.far):
                rows = pl.ds(pl.multiple_of((mine ^ offset) * piece, piece), piece)
                pltpu.make_async_copy(
                    source.at[pl.ds(matrix * piece, piece)],
                    self.target.at[matrix, rows],
                    self.semaphores.at[matrix],
                ).start()

    def wait(self, *order):
        for matrix in order:
            whole = self.target.at[matrix]
            pltpu.make_async_copy(whole, whole, self.semaphores.at[matrix]).wait()

    def __getitem__(self, matrix):
        return self.target[matrix]


def weight_scratch(width):
    return dict(
        weights=pltpu.VMEM((MATRICES, width, width), LOW),
        weight_semaphores=semaphores(MATRICES),
        vectors=pltpu.VMEM((EXTRA, width), LOW),
    )


def far_vectors(ref):
    return ref.far[0].at[pl.ds(ref.far[0].shape[0] - EXTRA, EXTRA)]


def project_nodes(spread, count, weights, vectors, joint):
    width = spread.shape[1]
    sender = 0.5 * dot_nn(spread, weights[SENDER_IN])
    middle = jnp.concatenate(
        [
            spread[start + count : start + 2 * count, :]
            for start in range(0, spread.shape[0], 3 * count)
        ],
        axis=0,
    )
    target = 0.5 * (dot_nn(middle, weights[TARGET_IN]) + vectors[0:1, :])
    half = weights[EDGE_IN] * 0.5
    for batch in range(spread.shape[0] // (3 * count)):
        joint[batch, :width, :] = half
        joint[batch, width : width + 3 * count, :] = sender[
            3 * count * batch : 3 * count * (batch + 1), :
        ].astype(LOW)
        joint[batch, width + 3 * count :, :] = target[
            count * batch : count * (batch + 1), :
        ].astype(LOW)
    return middle


def forward_tile(edges, hot_senders, hot_targets, joint, weights, vectors):
    joined = jnp.concatenate([edges, hot_senders, hot_targets], axis=1)
    active, slope = silu_parts(dot_nn(joined, joint))
    active = active.astype(LOW)
    unit, scale = norm_parts(dot_nn(active, weights[EDGE_OUT]) + vectors[1:2, :])
    return active, slope, unit, scale


def sum_updates(targets, units, vectors, count):
    hot = hot_rows(targets, count)
    degree = jnp.sum(hot.astype(F32), axis=1, keepdims=True)
    return vectors[2:3, :] * dot_nn(hot, units) + vectors[3:4, :] * degree


def node_forward(nodes, summed, weights, vectors):
    hidden = dot_nn(nodes, weights[NODE_IN]) + dot_nn(summed, weights[SUMMED_IN])
    active, slope = silu_parts(0.5 * (hidden + vectors[4:5, :]))
    active = active.astype(LOW)
    unit, scale = norm_parts(dot_nn(active, weights[NODE_OUT]) + vectors[5:6, :])
    states = nodes.astype(F32) + unit * vectors[6:7, :] + vectors[7:8, :]
    return states, active, slope, unit, scale


def node_backward(incoming, slope, unit, scale, weights, vectors):
    result_grad = norm_backward(incoming * vectors[6:7, :], unit, scale).astype(LOW)
    hidden_grad = (dot_nt(result_grad, weights[NODE_OUT]) * (0.5 * slope)).astype(LOW)
    base = incoming + dot_nt(hidden_grad, weights[NODE_IN])
    return result_grad, hidden_grad, base, dot_nt(hidden_grad, weights[SUMMED_IN])


def node_weight_grads(pack, nodes, summed, active, result_grad, hidden_grad, incoming, unit):
    width = nodes.shape[1]
    pack[:width, :] = dot_tn(nodes, hidden_grad).astype(LOW)
    pack[width : 2 * width, :] = dot_tn(summed, hidden_grad).astype(LOW)
    pack[2 * width : 3 * width, :] = dot_tn(active, result_grad).astype(LOW)
    sums = [
        column_sum(hidden_grad.astype(F32)),
        column_sum(result_grad.astype(F32)),
        column_sum(incoming * unit),
        column_sum(incoming),
    ]
    pack[3 * width :, :] = extra_rows(sums)


def extra_rows(sums):
    zeros = jnp.zeros((EXTRA - len(sums), sums[0].shape[1]), F32)
    return jnp.concatenate([*sums, zeros], axis=0).astype(LOW)


def backward_tile(incoming, slope, unit, scale, half_out, vectors):
    result_grad = norm_backward(incoming * vectors[2:3, :], unit, scale)
    low_grad = result_grad.astype(LOW)
    hidden_grad = (dot_nt(low_grad, half_out) * slope).astype(LOW)
    sums = (folded(result_grad), folded(incoming * unit), folded(incoming))
    return low_grad, hidden_grad, sums


def add_each(left, right):
    return tuple(a + b for a, b in zip(left, right))


def scattered(rows, hidden_grad, count):
    senders = dot_nn(hot_rows(rows[0:1, :], 3 * count), hidden_grad)
    targets = dot_nn(hot_rows(rows[1:2, :], count), hidden_grad)
    return senders, targets


def return_to_nodes(senders, targets, weights):
    count = targets.shape[0]
    grad = dot_nt(senders, weights[SENDER_IN])
    own = grad[count : 2 * count, :] + dot_nt(targets, weights[TARGET_IN])
    return grad[:count, :].astype(LOW), grad[2 * count :, :].astype(LOW), own


def send_pack(copies, row, pack, keep, send):
    half = (pack.shape[0] - EXTRA) // 2
    bit = row % 2
    for out, place in ((keep, bit), (send, 1 - bit)):
        rows = pl.ds(pl.multiple_of(place * half, half), half)
        copies.send(pack.at[rows], out.at[pl.ds(0, half)])
        copies.send(pack.at[pl.ds(2 * half, EXTRA)], out.at[pl.ds(half, EXTRA)])


def position_inputs(positions, halo, nodes, edges):
    return dict(rows=positions, spreads=(*halo, nodes), edges=edges)


def turned(rows):
    return jnp.transpose(rows.astype(F32)).astype(jnp.int32)


def spread_rows(ref, batch, count):
    odd = ref.place[1] % 2
    starts = ((3 * batch + 2 - 2 * odd) * count, (3 * batch + 2 * odd) * count)
    return [pl.ds(pl.multiple_of(start, count), count) for start in starts] + [
        pl.ds((3 * batch + 1) * count, count)
    ]


def fetch_spread(copies, ref, batches):
    count = ref.spreads[0].shape[1]
    return [
        copies.fetch(source.at[batch], ref.spread.at[rows])
        for batch in range(batches)
        for source, rows in zip(ref.spreads, spread_rows(ref, batch, count))
    ]


def by_parity(ref, below, above):
    odd = ref.place[1] % 2 == 1
    return jnp.where(odd, below, above), jnp.where(odd, above, below)


def layer_one(far, weights, place, positions, halo, nodes, edges):
    batches, count, width = nodes.shape
    slots = edges.shape[1]
    picked = batches
    chosen = range(batches)
    outputs = dict(
        states_low_out=shape((batches, count, width)), edges_out=shape((batches, slots, width))
    )
    if not far:
        outputs.update(
            states_out=shape((batches, count, width), F32),
            kept_out=shape((batches, 3, slots, width)),
            scales_out=shape((batches, slots, LANES), F32),
            node_kept_out=shape((batches, 3, count, width), F32),
            node_kept_low_out=shape((batches, 2, count, width)),
        )
    scratch = dict(
        **weight_scratch(width),
        joint=pltpu.VMEM((picked, 2 * width, width), LOW),
        spread=pltpu.VMEM((picked * 3 * count, width), LOW),
        edge_buffer=pltpu.VMEM((picked, slots, width), LOW),
        column_buffer=pltpu.VMEM((picked, slots, 8), jnp.int32),
        row_buffer=pltpu.VMEM((picked, 8, slots), jnp.int32),
        edges_new=pltpu.VMEM((picked, slots, width), LOW),
        summed=pltpu.VMEM((picked * count, width), LOW),
        states=pltpu.VMEM((picked, count, width), F32),
        states_low=pltpu.VMEM((picked, count, width), LOW),
        kept=pltpu.VMEM((picked, 3, slots, width), LOW),
        scales=pltpu.VMEM((picked, slots, LANES), F32),
        node_kept=pltpu.VMEM((picked, 3, count, width), F32),
        node_kept_low=pltpu.VMEM((picked, 2, count, width), LOW),
        semaphores=semaphores(48),
    )

    def work(ref):
        copies = Copies(ref.semaphores)
        weights = Weights(ref)
        first = [copies.fetch(far_vectors(ref) if far else ref.vectors_in, ref.vectors)]
        second = []
        first += fetch_spread(copies, ref, batches)
        fetch = weights.fetch_far if far else weights.fetch_near
        fetch(ref, ORDER[:3])
        for i, batch in enumerate(chosen):
            second.append(
                [
                    copies.fetch(ref.edges.at[batch], ref.edge_buffer.at[i]),
                    copies.fetch(ref.rows.at[batch], ref.row_buffer.at[i]),
                ]
            )
            if i == 0:
                fetch(ref, ORDER[3:])
        wait_all(first)
        vectors = ref.vectors[...].astype(F32)
        weights.wait(SENDER_IN, TARGET_IN, EDGE_IN)
        middle = project_nodes(ref.spread[...], count, weights, vectors, ref.joint)
        weights.wait(EDGE_OUT)
        for batch in range(batches):
            wait_all(second[batch])
            ref.column_buffer[batch] = turned(ref.row_buffer[batch])

        def edge_tile(batch, tile, _):
            index = ref.column_buffer[batch, tile, :]
            latents = ref.edge_buffer[batch, tile, :]
            active, slope, unit, scale = forward_tile(
                latents,
                hot_columns(index[:, 0:1], 3 * count),
                hot_columns(index[:, 1:2], count),
                ref.joint[batch],
                weights,
                vectors,
            )
            live = (index[:, 1:2] >= 0).astype(F32)
            update = (unit * vectors[2:3, :] + vectors[3:4, :]) * live
            ref.edges_new[batch, tile, :] = (latents.astype(F32) + update).astype(LOW)
            ref.kept[batch, 2, tile, :] = unit.astype(LOW)
            if not far:
                ref.kept[batch, 0, tile, :] = active
                ref.kept[batch, 1, tile, :] = slope.astype(LOW)
                ref.scales[batch, tile, :] = jnp.broadcast_to(scale, (TILE, LANES))

        def sum_batch(batch):
            targets = ref.row_buffer[batch, 1:2, :]
            summed = sum_updates(targets, ref.kept[batch, 2], vectors, count)
            ref.summed[block(batch, count), :] = summed.astype(LOW)

        if far:
            each_tile(batches, slots, edge_tile, True)
            repeat(batches, sum_batch, True)
        parts = slots // TILE
        for batch in range(batches):
            if not far:
                for part in range(parts):
                    edge_tile(batch, block(part, TILE), None)
            copies.send(ref.edges_new.at[batch], ref.edges_out.at[batch])
            if not far:
                copies.send(ref.kept.at[batch], ref.kept_out.at[batch])
                copies.send(ref.scales.at[batch], ref.scales_out.at[batch])
                sum_batch(batch)
        summed = ref.summed[...]
        weights.wait(NODE_IN, SUMMED_IN, NODE_OUT)
        states, active, slope, unit, scale = node_forward(middle, summed, weights, vectors)
        for i, batch in enumerate(chosen):
            rows = slice(i * count, (i + 1) * count)
            ref.states[i] = states[rows, :]
            ref.states_low[i] = states[rows, :].astype(LOW)
            copies.send(ref.states_low.at[i], ref.states_low_out.at[batch])
            if not far:
                copies.send(ref.states.at[i], ref.states_out.at[batch])
                ref.node_kept[i, 0] = slope[rows, :]
                ref.node_kept[i, 1] = unit[rows, :]
                ref.node_kept[i, 2] = jnp.broadcast_to(scale[rows, :], (count, width))
                ref.node_kept_low[i, 0] = summed[rows, :]
                ref.node_kept_low[i, 1] = active[rows, :]
                copies.send(ref.node_kept.at[i], ref.node_kept_out.at[batch])
                copies.send(ref.node_kept_low.at[i], ref.node_kept_low_out.at[batch])
        copies.finish()

    @run_kernel(
        place,
        dict(**weights, **position_inputs(positions, halo, nodes, edges)),
        outputs,
        scratch,
        section=1 if far else 0,
    )
    def layer_one_forward(ref):
        work(ref)

    return layer_one_forward


def layer_two(second, weights, place, positions, halo, nodes, edges, cotangent):
    batches, count, width = nodes.shape
    slots = edges.shape[1]
    every = batches * slots
    nodes_shape = (batches * count, width)
    outputs = dict(
        edge_low_out=shape((every, width)),
        base_out=shape(nodes_shape, F32),
        to_pair_out=shape(nodes_shape),
        to_other_out=shape(nodes_shape),
    )
    if second:
        outputs.update(
            states_out=shape(nodes_shape, F32),
            node_keep_out=shape((3 * width // 2 + EXTRA, width)),
            node_send_out=shape((3 * width // 2 + EXTRA, width)),
            edge_keep_out=shape((2 * width + EXTRA, width)),
            edge_send_out=shape((2 * width + EXTRA, width)),
        )
    all_low = pltpu.VMEM((every, width), LOW)
    scratch = dict(
        **weight_scratch(width),
        half_out=pltpu.VMEM((width, width), LOW),
        summed=pltpu.VMEM(nodes_shape, LOW),
        sums=pltpu.VMEM((3, 8, width), F32),
        senders=pltpu.VMEM((batches * 3 * count, width), LOW),
        targets=pltpu.VMEM(nodes_shape, F32),
        total=pltpu.VMEM((2, width, width), F32),
        joint=pltpu.VMEM((batches, 2 * width, width), LOW),
        spread=pltpu.VMEM((batches * 3 * count, width), LOW),
        edge_buffer=all_low,
        column_buffer=pltpu.VMEM((batches, slots, 8), jnp.int32),
        row_buffer=pltpu.VMEM((batches, 8, slots), jnp.int32),
        cotangent_buffer=pltpu.VMEM((batches * count, width), LOW),
        hot_targets=pltpu.VMEM((every, count), LOW),
        active_all=all_low,
        slope_all=all_low,
        unit_all=all_low,
        scales=pltpu.VMEM((every, LANES), F32),
        states=pltpu.VMEM(nodes_shape, F32),
        base=pltpu.VMEM(nodes_shape, F32),
        summed_grad=pltpu.VMEM(nodes_shape, LOW),
        result_grads=all_low,
        hidden_grads=all_low,
        edge_low=all_low,
        to_pair=pltpu.VMEM(nodes_shape, LOW),
        to_other=pltpu.VMEM(nodes_shape, LOW),
        node_pack=pltpu.VMEM((3 * width + EXTRA, width), LOW),
        edge_pack=pltpu.VMEM((4 * width + EXTRA, width), LOW),
        semaphores=semaphores(48),
    )
    inputs = dict(
        **weights, **position_inputs(positions, halo, nodes, edges), cotangent=cotangent
    )

    def work(ref):
        copies = Copies(ref.semaphores)
        weights = Weights(ref)
        first = [copies.fetch(ref.vectors_in if second else far_vectors(ref), ref.vectors)]
        first += fetch_spread(copies, ref, batches)
        fetch = weights.fetch_near if second else weights.fetch_far
        fetch(ref, ORDER[:3])
        loads = []
        for batch in range(batches):
            rows = pl.ds(batch * slots, slots)
            loads.append(
                [
                    copies.fetch(ref.edges.at[batch], ref.edge_buffer.at[rows]),
                    copies.fetch(ref.rows.at[batch], ref.row_buffer.at[batch]),
                ]
            )
            if batch == 0:
                fetch(ref, ORDER[3:])
        third = [
            copies.fetch(
                ref.cotangent.at[batch], ref.cotangent_buffer.at[pl.ds(batch * count, count)]
            )
            for batch in range(batches)
        ]
        wait_all(first)
        vectors = ref.vectors[...].astype(F32)
        weights.wait(SENDER_IN, TARGET_IN, EDGE_IN)
        middle = project_nodes(ref.spread[...], count, weights, vectors, ref.joint)
        weights.wait(EDGE_OUT)
        ref.half_out[...] = weights[EDGE_OUT] * 0.5
        for batch in range(batches):
            wait_all(loads[batch])
            ref.column_buffer[batch] = turned(ref.row_buffer[batch])

        def forward(batch, tile, place):
            index = ref.column_buffer[batch, tile, :]
            hot_targets = hot_columns(index[:, 1:2], count)
            active, slope, unit, scale = forward_tile(
                ref.edge_buffer[place, :],
                hot_columns(index[:, 0:1], 3 * count),
                hot_targets,
                ref.joint[batch],
                weights,
                vectors,
            )
            ref.hot_targets[place, :] = hot_targets
            if second:
                ref.active_all[place, :] = active
            ref.slope_all[place, :] = slope.astype(LOW)
            ref.unit_all[place, :] = unit.astype(LOW)
            ref.scales[place, :] = jnp.broadcast_to(scale, (TILE, LANES))

        def sum_batch(batch):
            units = ref.unit_all[block(batch, slots), :]
            targets = ref.row_buffer[batch, 1:2, :]
            summed = sum_updates(targets, units, vectors, count)
            ref.summed[block(batch, count), :] = summed.astype(LOW)

        each_tile(batches, slots, forward, 2 if second else 0)
        repeat(batches, sum_batch, second)
        summed = ref.summed[...]
        wait_all(third)
        weights.wait(NODE_IN, SUMMED_IN, NODE_OUT)
        states, active, slope, unit, scale = node_forward(middle, summed, weights, vectors)
        ref.states[...] = states
        incoming = ref.cotangent_buffer[...].astype(F32)
        result_grad, hidden_grad, base, summed_grad = node_backward(
            incoming, slope, unit, scale, weights, vectors
        )
        ref.summed_grad[...] = summed_grad.astype(LOW)
        ref.base[...] = base
        if second:
            node_weight_grads(
                ref.node_pack, middle, summed, active, result_grad, hidden_grad, incoming, unit
            )
        if second:
            ref.sums[...] = jnp.zeros_like(ref.sums)

        def backward(batch, tile, place):
            incoming = dot_nn(
                ref.hot_targets[place, :], ref.summed_grad[block(batch, count), :]
            )
            low_grad, hidden_grad, more = backward_tile(
                incoming,
                ref.slope_all[place, :].astype(F32),
                ref.unit_all[place, :].astype(F32),
                jnp.concatenate([ref.scales[place, :]] * (width // LANES), axis=1),
                ref.half_out[...],
                vectors,
            )
            edge_grad = dot_nt(hidden_grad, weights[EDGE_IN])
            if second:
                for i, item in enumerate(more):
                    ref.sums[i] += item
                ref.result_grads[place, :] = low_grad
            ref.hidden_grads[place, :] = hidden_grad
            ref.edge_low[place, :] = edge_grad.astype(LOW)

        def scatter(batch):
            rows = block(batch, slots)
            here = block(batch, count)
            to_senders, to_targets = scattered(
                ref.row_buffer[batch], ref.hidden_grads[rows, :], count
            )
            to_senders = to_senders.astype(LOW)
            if second:
                ref.senders[block(batch, 3 * count), :] = to_senders
                ref.targets[here, :] = to_targets
            below, above, own = return_to_nodes(to_senders, to_targets.astype(LOW), weights)
            below, above = by_parity(ref, below, above)
            ref.to_pair[here, :] = below
            ref.to_other[here, :] = above
            ref.base[here, :] += own

        parts = slots // TILE
        if second:
            each_tile(batches, slots, backward, True)
            copies.send(ref.edge_low, ref.edge_low_out)
            repeat(batches, scatter, True)
        for batch in range(0 if second else batches):
            for part in range(parts):
                backward(batch, None, block(batch * parts + part, TILE))
            rows = block(batch, slots)
            copies.send(ref.edge_low.at[rows], ref.edge_low_out.at[rows])
            scatter(batch)
        copies.send(ref.to_pair, ref.to_pair_out)
        copies.send(ref.to_other, ref.to_other_out)
        copies.send(ref.base, ref.base_out)
        if second:
            copies.send(ref.states, ref.states_out)
            ref.total[...] = jnp.zeros_like(ref.total)

            def add_rows(i):
                rows = block(i, TILE)
                ref.total[0] += dot_tn(ref.edge_buffer[rows, :], ref.hidden_grads[rows, :])
                ref.total[1] += dot_tn(ref.active_all[rows, :], ref.result_grads[rows, :])

            repeat(every // TILE, add_rows, True)
            edge_weight_grads(
                ref.edge_pack,
                ref.total[0],
                ref.total[1],
                ref.spread[...],
                middle,
                ref.senders[...],
                ref.targets[...],
                [ref.sums[i] for i in range(3)],
            )
            send_pack(copies, ref.place[1], ref.edge_pack, ref.edge_keep_out, ref.edge_send_out)
            send_pack(copies, ref.place[1], ref.node_pack, ref.node_keep_out, ref.node_send_out)
        copies.finish()

    @run_kernel(place, inputs, outputs, scratch, work=6.0, section=1 if second else 0)
    def layer_two_both(ref):
        work(ref)

    return layer_two_both


def edge_weight_grads(pack, edge_part, active_part, spread, middle, senders, targets, sums):
    width = spread.shape[1]
    pack[:width, :] = edge_part.astype(LOW)
    pack[width : 2 * width, :] = dot_tn(spread, senders).astype(LOW)
    pack[2 * width : 3 * width, :] = dot_tn(middle, targets.astype(LOW)).astype(LOW)
    pack[3 * width : 4 * width, :] = active_part.astype(LOW)
    pack[4 * width :, :] = extra_rows([column_sum(targets), *map(column_sum, sums)])


def layer_one_back(weights, place, positions, halo, nodes, edges, near, two, packs, second):
    batches, count, width = nodes.shape
    slots = edges.shape[1]
    every = batches * slots
    nodes_shape = (batches * count, width)
    loaded = dict(
        base=second[0],
        from_pair=second[1],
        from_other=second[2],
        node_kept=near.node_kept_out,
        node_kept_low=near.node_kept_low_out,
    )
    outputs = dict(hidden_out=shape((every, width)))
    all_low = pltpu.VMEM((every, width), LOW)
    nodes_low = pltpu.VMEM(nodes_shape, LOW)
    scratch = dict(
        **weight_scratch(width),
        half_out=pltpu.VMEM((width, width), LOW),
        spread=pltpu.VMEM((batches * 3 * count, width), LOW),
        edge_buffer=all_low,
        column_buffer=pltpu.VMEM((batches, slots, 8), jnp.int32),
        row_buffer=pltpu.VMEM((batches, 8, slots), jnp.int32),
        kept=pltpu.VMEM((3, every, width), LOW),
        scales=pltpu.VMEM((every, LANES), F32),
        edge_low=all_low,
        summed_grad=nodes_low,
        to_pair=nodes_low,
        to_other=nodes_low,
        result_grads=all_low,
        hidden_grads=all_low,
        node_pack=pltpu.VMEM((3 * width + EXTRA, width), LOW),
        edge_pack=pltpu.VMEM((4 * width + EXTRA, width), LOW),
        semaphores=semaphores(64),
        **{key: pltpu.VMEM(value.shape, value.dtype) for key, value in loaded.items()},
    )
    renewed = dict(
        node_keep_out=packs.node_keep_out,
        node_send_out=packs.node_send_out,
        edge_keep_out=packs.edge_keep_out,
        edge_send_out=packs.edge_send_out,
        base_out=packs.base_out,
        to_pair_out=packs.to_pair_out,
        to_other_out=packs.to_other_out,
    )
    inputs = dict(
        **weights,
        **position_inputs(positions, halo, nodes, edges),
        loads=tuple(loaded.values()),
        edge_low_in=two.edge_low_out,
        scales_in=near.scales_out,
        kept_in=near.kept_out,
    )

    def stacked(items):
        return jnp.concatenate(items, axis=0)

    def work(ref):
        copies = Copies(ref.semaphores)
        weights = Weights(ref)
        first = [copies.fetch(ref.vectors_in, ref.vectors)]
        first += [copies.fetch(source, getattr(ref, key)) for key, source in zip(loaded, ref.loads)]
        weights.fetch_near(ref, (NODE_OUT, NODE_IN, SUMMED_IN))
        first += fetch_spread(copies, ref, batches)
        second = []
        third = []
        for batch in range(batches):
            rows = pl.ds(batch * slots, slots)
            second.append(
                [
                    copies.fetch(ref.edge_low_in.at[rows], ref.edge_low.at[rows]),
                    copies.fetch(ref.scales_in.at[batch], ref.scales.at[rows]),
                    copies.fetch(ref.kept_in.at[batch], ref.kept.at[:, rows]),
                    copies.fetch(ref.rows.at[batch], ref.row_buffer.at[batch]),
                ]
            )
            if batch == 0:
                weights.fetch_near(ref, (EDGE_OUT, SENDER_IN, TARGET_IN))
            third.append(copies.fetch(ref.edges.at[batch], ref.edge_buffer.at[rows]))
        wait_all(first)
        vectors = ref.vectors[...].astype(F32)
        weights.wait(NODE_OUT, NODE_IN, SUMMED_IN)
        middle = stacked(
            [
                ref.spread[(3 * batch + 1) * count : (3 * batch + 2) * count, :]
                for batch in range(batches)
            ]
        )
        incoming = (
            ref.base[...] + ref.from_pair[...].astype(F32) + ref.from_other[...].astype(F32)
        )
        incoming = incoming.astype(LOW).astype(F32)
        slope, unit, scale = (
            stacked([ref.node_kept[batch, i] for batch in range(batches)]) for i in range(3)
        )
        summed, active = (
            stacked([ref.node_kept_low[batch, i] for batch in range(batches)]) for i in range(2)
        )
        result_grad, hidden_grad, base, summed_grad = node_backward(
            incoming, slope, unit, scale, weights, vectors
        )
        ref.summed_grad[...] = summed_grad.astype(LOW)
        ref.base[...] = base
        node_weight_grads(
            ref.node_pack, middle, summed, active, result_grad, hidden_grad, incoming, unit
        )
        weights.wait(EDGE_OUT, SENDER_IN, TARGET_IN)
        ref.half_out[...] = weights[EDGE_OUT] * 0.5
        sums = None
        senders = []
        targets = []
        for batch in range(batches):
            wait_all(second[batch])
            ref.column_buffer[batch] = turned(ref.row_buffer[batch])
            nodes_here = slice(batch * count, (batch + 1) * count)
            for part in range(slots // TILE):
                tile, place = block(part, TILE), block(batch * (slots // TILE) + part, TILE)
                hot = hot_columns(ref.column_buffer[batch, tile, 1:2], count)
                incoming = ref.edge_low[place, :].astype(F32) + dot_nn(
                    hot, ref.summed_grad[nodes_here, :]
                )
                low_grad, hidden_grad, more = backward_tile(
                    incoming,
                    ref.kept[1, place, :].astype(F32),
                    ref.kept[2, place, :].astype(F32),
                    jnp.concatenate([ref.scales[place, :]] * (width // LANES), axis=1),
                    ref.half_out[...],
                    vectors,
                )
                sums = more if sums is None else add_each(sums, more)
                ref.result_grads[place, :] = low_grad
                ref.hidden_grads[place, :] = hidden_grad
            rows = slice(batch * slots, (batch + 1) * slots)
            to_senders, to_targets = scattered(
                ref.row_buffer[batch], ref.hidden_grads[rows, :], count
            )
            senders.append(to_senders.astype(LOW))
            targets.append(to_targets)
        wait_all(third)
        copies.send(ref.hidden_grads, ref.hidden_out)
        edge_weight_grads(
            ref.edge_pack,
            dot_tn(ref.edge_buffer[...], ref.hidden_grads[...]),
            dot_tn(ref.kept[0], ref.result_grads[...]),
            ref.spread[...],
            middle,
            stacked(senders),
            stacked(targets),
            sums,
        )
        send_pack(copies, ref.place[1], ref.edge_pack, ref.edge_keep_out, ref.edge_send_out)
        send_pack(copies, ref.place[1], ref.node_pack, ref.node_keep_out, ref.node_send_out)
        for batch in range(batches):
            nodes_here = slice(batch * count, (batch + 1) * count)
            below, above, own = return_to_nodes(
                senders[batch], targets[batch].astype(LOW), weights
            )
            below, above = by_parity(ref, below, above)
            ref.to_pair[nodes_here, :] = below
            ref.to_other[nodes_here, :] = above
            ref.base[nodes_here, :] += own
        copies.send(ref.to_pair, ref.to_pair_out)
        copies.send(ref.to_other, ref.to_other_out)
        copies.send(ref.base, ref.base_out)
        copies.finish()

    @run_kernel(place, inputs, outputs, scratch, renewed=renewed, work=6.0)
    def layer_one_backward(ref):
        pl.when(ref.place[0] == 0)(lambda: work(ref))

    return layer_one_backward


def edge_outputs(weights, place, near_low, far_low, hidden, after):
    every, width = near_low.shape
    scratch = dict(
        edge_weight=pltpu.VMEM((width, width), LOW),
        edge_buffer=pltpu.VMEM((every, width), LOW),
        hidden_buffer=pltpu.VMEM((every, width), LOW),
        full=pltpu.VMEM((every, width), F32),
        semaphores=semaphores(2 * every // TILE + every // TILE + 1),
    )

    @run_kernel(
        place,
        dict(
            edge_in=weights["edge_in"],
            near_low=near_low,
            far_low=far_low,
            hidden=hidden,
        ),
        dict(edge_grads_out=shape((every, width), F32)),
        scratch,
        work=0.05,
        after=after,
    )
    def edge_gradients(ref):
        first_section = ref.place[0] == 0
        copies = Copies(ref.semaphores)
        weight = copies.fetch(ref.edge_in.at[0], ref.edge_weight)
        arriving = [
            [
                copies.fetch(ref.hidden.at[tile], ref.hidden_buffer.at[tile]),
                copies.fetch_either(
                    first_section,
                    ref.near_low.at[tile],
                    ref.far_low.at[tile],
                    ref.edge_buffer.at[tile],
                ),
            ]
            for tile in [block(i, TILE) for i in range(every // TILE)]
        ]
        weight.wait()
        for tile, loads in zip([block(i, TILE) for i in range(every // TILE)], arriving):
            wait_all(loads)
            edge_in = ref.edge_buffer[tile, :].astype(F32)

            @pl.when(ref.place[0] == 0)
            def _():
                more = dot_nt(ref.hidden_buffer[tile, :], ref.edge_weight[...])
                ref.full[tile, :] = edge_in + more

            @pl.when(ref.place[0] == 1)
            def _():
                ref.full[tile, :] = edge_in

            copies.send(ref.full.at[tile], ref.edge_grads_out.at[tile])
        copies.finish()

    return edge_gradients.edge_grads_out, edge_gradients.token


def node_outputs(place, near, far_two, back, received, after):
    dims = far_two.states_out.shape
    full = pltpu.VMEM(dims, F32)
    low = pltpu.VMEM(dims, LOW)

    @run_kernel(
        place,
        dict(
            parts=(back.base_out, *received),
            near=near.states_out.reshape(dims),
            far=far_two.states_out,
        ),
        dict(grads_out=shape(dims, F32), states_out=shape(dims, F32)),
        dict(base=full, below=low, above=low, states=full, semaphores=semaphores(6)),
        work=0.02,
        after=after,
    )
    def finish_nodes(ref):
        first_section = ref.place[0] == 0
        copies = Copies(ref.semaphores)
        states = copies.fetch_either(first_section, ref.near, ref.far, ref.states)
        wait_all(
            [copies.fetch(*pair) for pair in zip(ref.parts, (ref.base, ref.below, ref.above))]
        )
        total = ref.base[...] + ref.below[...].astype(F32) + ref.above[...].astype(F32)
        ref.base[...] = jnp.where(first_section, total, total.astype(LOW).astype(F32))
        copies.send(ref.base, ref.grads_out)
        states.wait()
        copies.send(ref.states, ref.states_out)
        copies.finish()

    return finish_nodes


def weight_pieces(weights, vectors, place):
    width = weights["edge_out"].shape[1]
    piece = width // PIECES
    rows = MATRICES * piece + EXTRA

    @run_kernel(
        place,
        dict(**weights, lines=vectors),
        dict(
            own_out=shape((rows, width)),
            other_out=shape((rows, width)),
            vectors_out=shape((EXTRA, width)),
        ),
        dict(
            own=pltpu.VMEM((rows, width), LOW),
            other=pltpu.VMEM((rows, width), LOW),
            single=pltpu.VMEM((len(vectors), 1, width), LOW),
            semaphores=semaphores(2 * MATRICES + len(vectors) + 3),
        ),
        work=0.02,
    )
    def weight_piece(ref):
        copies = Copies(ref.semaphores)
        mine = ref.place[1] % PIECES
        sources = near_sources(ref)
        lines = [copies.fetch(line, ref.single.at[i]) for i, line in enumerate(ref.lines)]
        arriving = []
        for buffer, offset in ((ref.own, 0), (ref.other, 6)):
            place = pl.ds(pl.multiple_of((mine ^ offset) * piece, piece), piece)
            for matrix, source in enumerate(sources):
                target = buffer.at[pl.ds(matrix * piece, piece)]
                arriving.append(copies.fetch(source.at[place], target))
        wait_all(lines)
        extra = extra_rows([ref.single[i].astype(F32) for i in range(len(lines))])
        for buffer in (ref.own, ref.other):
            buffer[MATRICES * piece :, :] = extra
        wait_all(arriving)
        copies.send(ref.own, ref.own_out)
        copies.send(ref.other, ref.other_out)
        copies.send(ref.own.at[pl.ds(MATRICES * piece, EXTRA)], ref.vectors_out)
        copies.finish()

    return weight_piece


def along_rows(value, route):
    length = lax.axis_size("rows")
    return lax.ppermute(value, "rows", [(i, route(i)) for i in range(length)])


def neighbours(value, section=None, other=None):
    length = lax.axis_size("rows")
    pair = [(i, i ^ 1) for i in range(length)]
    beside = [(i, (i + 1 if i % 2 else i - 1) % length) for i in range(length)]
    axes = "rows"
    if section is not None:
        axes = ("section", "rows")
        start = section * length
        pair, beside = (
            [(start + one, start + two) for one, two in pairs] for pairs in (pair, beside)
        )
    return (
        lax.ppermute(value, axes, pair),
        lax.ppermute(value if other is None else other, axes, beside),
    )


def across(value, mask):
    return along_rows(value, lambda i: i ^ mask)


def exchange(value, stage):
    return along_rows(value, lambda i: i ^ (1 << stage[i % 2]))


def stage_bit(row, stage):
    return (row >> jnp.where(row % 2 == 0, stage[0], stage[1])) & 1


def add_part(kept, received, place, stage, other, after=None):
    rows, width = kept.shape
    half = (rows - EXTRA) // 2

    @run_kernel(
        place,
        {},
        {},
        {},
        near_inputs=dict(kept=kept, received=received),
        near_outputs=dict(sum_out=shape((half + EXTRA, width))),
        work=0.01,
        memory=8,
        after=after,
    )
    def add_halves(ref):
        bit = stage_bit(ref.place[1], stage)
        part = pl.ds(pl.multiple_of((1 - bit if other else bit) * half, EXTRA), half)
        total = ref.kept[part, :].astype(F32) + ref.received[part, :].astype(F32)
        ref.sum_out[:half, :] = total.astype(LOW)
        total = ref.kept[2 * half :, :].astype(F32) + ref.received[2 * half :, :].astype(F32)
        ref.sum_out[half:, :] = total.astype(LOW)

    return add_halves


def add_last(kept, received, place, after):
    rows, width = kept.shape
    rows = rows - EXTRA

    @run_kernel(
        place,
        {},
        {},
        {},
        near_inputs=dict(kept=kept, received=received),
        near_outputs=dict(own_out=shape((rows, width)), extra_out=shape((EXTRA, width), F32)),
        work=0.01,
        memory=8,
        after=after,
    )
    def add_chunk(ref):
        total = ref.kept[...].astype(F32) + ref.received[...].astype(F32)
        ref.own_out[...] = total[:rows, :].astype(LOW)
        ref.extra_out[...] = total[rows:, :]

    return add_chunk


def join(own, received, place, stage, after):
    rows, width = own.shape

    @run_kernel(
        place,
        {},
        {},
        {},
        near_inputs=dict(own=own, received=received),
        near_outputs=dict(joined_out=shape((2 * rows, width))),
        work=0.01,
        memory=8,
        after=after,
    )
    def join_halves(ref):
        bit = stage_bit(ref.place[1], stage)
        for source, side in ((ref.own, bit), (ref.received, 1 - bit)):
            ref.joined_out[pl.ds(pl.multiple_of(side * rows, EXTRA), rows), :] = source[...]

    return join_halves


def unpack(pairs, place, stage, flipped, previous, extras=()):
    width = pairs[0][0].shape[1]
    quarters = [pair[0].shape[0] for pair in pairs]
    renewed = {}
    outputs = {}
    for i, quarter in enumerate(quarters):
        outputs[f"inner_{i}"] = shape((4 * quarter - width, width), F32)
        outputs[f"outer_{i}"] = shape((width, width), F32)
    if previous is not None:
        renewed = {key: getattr(previous, key) for key in outputs}
        outputs = {}
    lines = {f"line_{i}": shape((1, width), F32) for i in range(4 * len(extras))}
    chunks = tuple(chunk for pair in pairs for chunk in pair)

    @run_kernel(
        place,
        {},
        outputs,
        dict(
            full=pltpu.VMEM((2 * sum(quarters), width), F32),
            semaphores=semaphores(4 * len(pairs)),
        ),
        near_inputs=dict(chunks=chunks, extras=extras),
        near_outputs=lines,
        renewed=renewed,
        work=0.02,
        memory=16,
        after=(),
    )
    def widen_sums(ref):
        for i in range(len(lines)):
            getattr(ref, f"line_{i}")[...] = ref.extras[i // 4][i % 4 : i % 4 + 1, :]
        step = EXTRA * 8
        moves = []
        base = 0
        for i, chunk in enumerate(ref.chunks):
            quarter = chunk.shape[0]
            for row in range(0, quarter, step):
                ref.full[base + row : base + row + step, :] = chunk[row : row + step, :].astype(F32)
            row = ref.place[1] ^ (i % 2)
            found = 2 * (row % 2) + (stage_bit(row, stage) ^ flipped)
            middle = 4 * quarter - width
            for place in range(4):
                first, last = place * quarter, (place + 1) * quarter
                copies = []
                for j, (out, start, stop, offset) in enumerate(
                    (
                        (getattr(ref, f"inner_{i // 2}"), first, min(last, middle), 0),
                        (getattr(ref, f"outer_{i // 2}"), max(first, middle), last, middle),
                    )
                ):
                    if start < stop:
                        copies.append(
                            pltpu.make_async_copy(
                                ref.full.at[pl.ds(base + start - first, stop - start)],
                                out.at[pl.ds(start - offset, stop - start)],
                                ref.semaphores.at[2 * i + j],
                            )
                        )
                moves.append((found == place, copies))
            base += quarter
        for here, copies in moves:

            @pl.when(here)
            def _():
                for copy in copies:
                    copy.start()

        for here, copies in moves:
            pl.when(here)(lambda: wait_all(copies))

    return widen_sums


def held_back(arrays, place, before):
    keys = [f"array_{i}" for i in range(len(arrays))]

    @run_kernel(
        place,
        dict(before=before),
        {},
        {},
        renewed=dict(zip(keys, arrays.values())),
        work=0.01,
        memory=8,
    )
    def pass_on(ref):
        pass

    return {key: getattr(pass_on, name) for key, name in zip(arrays, keys)}


class RowSum:
    def __init__(self, keep, send, place, row):
        length = lax.axis_size("rows")
        bits = length.bit_length() - 1
        self.keep, self.send, self.place, self.row = keep, send, place, row
        self.half = keep.shape[0] - EXTRA
        self.direct = length == 1 << bits and (self.half >> (bits - 1)) % EXTRA == 0
        self.stages = [(0, 0), (1, 2), (2, 1)] + [(i, i) for i in range(3, bits)]
        if self.direct:
            self.received = exchange(send, self.stages[0])

    def halve(self, stage, *after):
        sent = add_part(self.keep, self.received, self.place, stage, 1, after)
        received = exchange(sent.sum_out, stage)
        self.keep = add_part(self.keep, self.received, self.place, stage, 0).sum_out
        self.received = received
        return sent.token

    def turn(self, *after):
        chunk = add_last(self.keep, self.received, self.place, after)
        self.own, self.extra = chunk.own_out, chunk.extra_out
        self.received = exchange(self.own, self.stages[-1])
        return chunk.token

    def double(self, stage, following, *after):
        joined = join(self.own, self.received, self.place, stage, after)
        self.own = joined.joined_out
        self.received = exchange(self.own, following)
        return joined.token

    def plain(self):
        width = self.keep.shape[1]
        even = self.row % 2 == 0
        pack = [jnp.where(even, self.keep, self.send)[: self.half]]
        pack.append(jnp.where(even, self.send, self.keep))
        total = lax.psum(jnp.concatenate(pack, axis=0), "rows").astype(F32)
        inner, outer, extra = jnp.split(total, (2 * self.half - width, 2 * self.half))
        return inner, outer, [extra[i : i + 1] for i in range(4)]


def sum_streams(streams, fillers):
    if not all(stream.direct for stream in streams):
        for filler in fillers:
            filler(())
        return [stream.plain() for stream in streams]
    stages = streams[0].stages
    mark = ()
    for i, stage in enumerate(stages[1:]):
        for stream in streams:
            mark = (stream.halve(stage, *mark),)
        if i == 2:
            mark = fillers[0](mark)
    for stream in streams[::-1]:
        mark = (stream.turn(*mark),)
    mark = fillers[1](mark)
    for stage, following in zip(stages[:1:-1], stages[-2:0:-1]):
        for stream in streams[::-1]:
            mark = (stream.double(stage, following, *mark),)
    place = streams[0].place
    extras = tuple(stream.extra for stream in streams)
    known = [(stream.own, exchange(stream.own, stages[0])) for stream in streams]
    first = unpack(known, place, stages[1], 0, None, extras)
    late = held_back({i: stream.received for i, stream in enumerate(streams)}, place, first.token)
    rest = [(late[i], exchange(late[i], stages[0])) for i in range(len(streams))]
    both = unpack(rest, place, stages[1], 1, first)
    return [
        (
            getattr(both, f"inner_{i}"),
            getattr(both, f"outer_{i}"),
            [getattr(first, f"line_{4 * i + j}") for j in range(4)],
        )
        for i in range(len(streams))
    ]


def per_device(
    node_latents,
    edge_latents,
    senders,
    receivers,
    cotangent,
    edge_weight_in,
    edge_bias_in,
    edge_weight_out,
    edge_bias_out,
    edge_gain,
    edge_shift,
    node_weight_in,
    node_bias_in,
    node_weight_out,
    node_bias_out,
    node_gain,
    node_shift,
):
    batches, count, width = node_latents.shape
    total = count * lax.axis_size("rows")
    row = lax.axis_index("rows")
    start = row * count
    place = jnp.stack([lax.axis_index("section"), row]).astype(jnp.int32)

    weights = dict(
        edge_in=edge_weight_in.reshape(3, width, width),
        edge_out=edge_weight_out[0],
        node_in=node_weight_in.reshape(2, width, width),
        node_out=node_weight_out[0],
    )
    vectors = (
        edge_bias_in,
        edge_bias_out,
        edge_gain,
        edge_shift,
        node_bias_in,
        node_bias_out,
        node_gain,
        node_shift,
    )
    swap = [(0, 1), (1, 0)]
    pieces = weight_pieces(weights, vectors, place)
    halo = neighbours(node_latents)
    near = dict(**weights, vectors_in=pieces.vectors_out)
    straight = lax.ppermute(pieces.own_out, "section", swap)
    crossed = lax.ppermute(pieces.other_out, "section", swap)

    live = receivers >= 0
    targets = jnp.where(live, receivers - start, -1)
    sources = jnp.where(live, jnp.mod(senders - start + count, total), -1)
    positions = jnp.pad(jnp.stack([sources, targets], axis=1), ((0, 0), (0, 6), (0, 0)))

    near_run = layer_one(False, near, place, positions, halo, node_latents, edge_latents)
    near_low = near_run.states_low_out
    first = held_back({0: straight}, place, near_low)[0]
    found = {0: first, 6: crossed, 2: across(first, 2), 4: across(first, 4)}
    near_halo = neighbours(near_low, 0)
    found.update(held_back({key: found[key] for key in (2, 4)}, place, near_halo))
    for offset in list(found):
        found[offset ^ 1] = across(found[offset], 1)
    far = dict(far=tuple(found[offset] for offset in range(PIECES)))
    near_two = layer_two(
        False,
        far,
        place,
        positions,
        near_halo,
        near_low,
        near_run.edges_out,
        cotangent,
    )
    after_near = dict(**far, first=near_two.base_out)
    one = layer_one(True, after_near, place, positions, halo, node_latents, edge_latents)
    far_low = one.states_low_out
    far_two = layer_two(
        True,
        near,
        place,
        positions,
        neighbours(far_low, 1),
        far_low,
        one.edges_out,
        cotangent,
    )
    second = (near_two.base_out, *neighbours(near_two.to_pair_out, 0, near_two.to_other_out))
    back = layer_one_back(
        near,
        place,
        positions,
        halo,
        node_latents,
        edge_latents,
        near_run,
        near_two,
        far_two,
        second,
    )
    received = neighbours(back.to_pair_out, None, back.to_other_out)
    late = {}

    def finish_nodes(mark):
        late["nodes"] = node_outputs(
            place, near_run, far_two, back, received, mark
        )
        return (late["nodes"].token,)

    def finish_edges(mark):
        late["grads"], token = edge_outputs(
            near,
            place,
            near_two.edge_low_out,
            far_two.edge_low_out,
            back.hidden_out,
            mark,
        )
        return (token,)

    edge_sums, node_sums = sum_streams(
        [
            RowSum(back.edge_keep_out, back.edge_send_out, place, row),
            RowSum(back.node_keep_out, back.node_send_out, place, row),
        ],
        (finish_edges, finish_nodes),
    )
    lines = [line for sums in (edge_sums, node_sums) for line in sums[2]]
    return (
        late["nodes"].states_out.reshape(halo[0].shape)[None],
        late["nodes"].grads_out.reshape(halo[0].shape)[None],
        late["grads"].reshape(edge_latents.shape)[None],
        edge_sums[0][None],
        lines[0],
        edge_sums[1][None],
        *lines[1:4],
        node_sums[0][None],
        lines[4],
        node_sums[1][None],
        *lines[5:],
    )


def solution(mesh):
    batch_rows = P(None, "rows", None)
    matrix = P("section", None, None)
    vector = P("section", None)
    by_layer = P("section", None, "rows", None)
    weights = (matrix, vector, matrix, vector, vector, vector)
    in_specs = (batch_rows, batch_rows, P(None, "rows"), P(None, "rows"), batch_rows)
    return jax.shard_map(
        per_device,
        mesh=mesh,
        in_specs=in_specs + weights + weights,
        out_specs=(by_layer,) * 3 + weights + weights,
        check_vma=False,
    )
```
